256 devices in a mesh: rows: 8 (over x, core), vocab: 32 (over y, z).
Axes of the slice: x: 4, y: 4, z: 8, core: 2. Of those that a mesh axis runs over, the one named last changes fastest.
Arguments:
- hidden: bfloat16 [1536, 8192], P(None, 'rows'), may hold values from -32 to 32
- table: bfloat16 [65536, 8192], P('vocab', 'rows'), may hold values from -0.5 to 0.5
- subset_ids: int32 [32768], P('vocab'), may hold values from 0 to 65535, as said below
- targets: bfloat16 [1536, 32768], P('rows', 'vocab'), may hold values from 0 to 1, as said below
Outputs:
- draft_logits: bfloat16 [1536, 32768], P('rows', 'vocab')
- hidden_grad: bfloat16 [1536, 8192], P('vocab', 'rows')
- table_grad: bfloat16 [65536, 8192], P('vocab', 'rows')
The draws below stay inside these ranges and needn't reach their ends.
Inputs may be any that keep to these rules, and one draw needn't show every extreme that they name: `subset_ids`: all ids differ. Table shard o holds ids o * 2048 to (o + 1) * 2048 - 1. Among the 1024 ids of one vocab shard, a quarter of the table shards hold 64 each, a quarter 64 / 2 each and the other half 64 / 4 each; one table shard holds 64 ids of every vocab shard. `targets`: Positive.
All inputs are finite; a program needn't handle non-finite values.
Results may differ from the reference program's by a relative error of at most 0.0049.
Values may be sent and summed in bfloat16 or wider, within the bound.
No kernel may reach another device: no remote copies, remote signals or barrier semaphores. Data moves between devices by JAX's collectives and lax.ppermute only.
A program may use at most 128 MiB of HBM per device.

```python
import math
import jax
import jax.numpy as jnp

D = 8192
VF_DEV = 2048
SUB_DEV = 1024
VF = 65536
S = 32768
P_SIZE = 1536


def subset_layout(key):
    key = jax.random.fold_in(key, 101)
    shards = S // SUB_DEV
    capacity = 2 * SUB_DEV // shards
    quarter = shards // 4
    places = jnp.arange(shards)
    profile = jnp.where(places < quarter, capacity, jnp.where(places < 2 * quarter, capacity // 2, capacity // 4)).astype(jnp.int32)
    hottest = jax.random.randint(jax.random.fold_in(key, 1), (), 0, shards, dtype=jnp.int32)
    scores = jax.random.randint(jax.random.fold_in(key, 2), (shards, shards), 0, 2 ** 18, dtype=jnp.int32) * shards + places[None, :].astype(jnp.int32)
    scores = jnp.where(places[None, :] == hottest, -1, scores)
    order = jnp.argsort(scores, axis=1).astype(jnp.int32)
    shard_index = jnp.arange(shards)[:, None]
    counts = jnp.zeros((shards, shards), jnp.int32).at[shard_index, order].set(jnp.broadcast_to(profile[None, :], (shards, shards)))
    offsets = jnp.cumsum(counts, axis=0) - counts
    ends = jnp.cumsum(profile)
    starts = ends - profile
    slots = jnp.arange(SUB_DEV).astype(jnp.int32)
    position = jnp.sum((slots[:, None] >= ends[None, :]).astype(jnp.int32), axis=1)
    within = slots - starts[position]
    owner_of = order[:, position]
    slot_rank = offsets[shard_index, owner_of] + within[None, :]
    own_scores = jax.random.randint(jax.random.fold_in(key, 3), (shards, VF_DEV), 0, 2 ** 18, dtype=jnp.int32) * VF_DEV + jnp.arange(VF_DEV).astype(jnp.int32)[None, :]
    own_scores = own_scores.at[:, VF_DEV - 1].set(-2).at[:, 0].set(-1)
    own_order = jnp.argsort(own_scores, axis=1).astype(jnp.int32)
    local_row = own_order[owner_of, slot_rank]
    ids = owner_of * VF_DEV + local_row
    shuffle_scores = jax.random.randint(jax.random.fold_in(key, 4), (shards, SUB_DEV), 0, 2 ** 18, dtype=jnp.int32) * SUB_DEV + slots[None, :]
    shuffle = jnp.argsort(shuffle_scores, axis=1)
    ids = jnp.take_along_axis(ids, shuffle, axis=1)
    return ids.reshape(S).astype(jnp.int32)


def table_rows(key, rows):
    key = jax.random.fold_in(key, 202)
    scale = 3.0 / math.sqrt(D)

    def one_row(index):
        values = jax.random.normal(jax.random.fold_in(key, index), (D,), jnp.float32)
        return jnp.clip(jnp.clip(values, -6.0, 6.0) * scale, -0.5, 0.5)
    return jax.vmap(one_row)(rows)


def draw_subset_ids(key, part):
    return subset_layout(key)


def draw_table(key, part):
    base = table_rows(key, jnp.arange(VF).astype(jnp.int32))
    return base.astype(jnp.bfloat16)


def draw_hidden(key, part):
    ids = subset_layout(key)
    own_key = jax.random.fold_in(key, 9)
    base = jnp.clip(jax.random.normal(own_key, (P_SIZE, D), jnp.float32), -6.0, 6.0)
    picks = jax.random.randint(jax.random.fold_in(own_key, 1), (P_SIZE, 2), 0, S, dtype=jnp.int32)
    first = jnp.sign(table_rows(key, ids[picks[:, 0]]))
    second = jnp.sign(table_rows(key, ids[picks[:, 1]]))
    level = jnp.array([120.0, 170.0, 240.0], jnp.float32)[jnp.arange(P_SIZE) % 3]
    strength = level / (2.4 * math.sqrt(D))
    aligned = jnp.clip(strength[:, None] * (first + 0.9 * second), -32.0, 32.0)
    chosen = (jnp.arange(P_SIZE) % 8 == 0)[:, None]
    values = jnp.where(chosen, aligned, base)
    return values.astype(jnp.bfloat16)


def draw_targets(key, part):
    key = jax.random.fold_in(key, 5)
    ranks = jnp.arange(S).astype(jnp.float32) / S
    noise = jnp.clip(jax.random.normal(key, (P_SIZE, S), jnp.float32), -4.5, 4.5)
    decay = jnp.exp(-1.5 * ranks)
    norm = 0.7 / (90.0 * S * 0.518)
    values = jnp.minimum(jnp.exp(3.0 * noise) * decay[None, :] * norm, 1.0)
    return values.astype(jnp.bfloat16)


def setup_inputs(seed: int = 0) -> dict:
    arg_keys = jax.random.split(jax.random.key(seed), 5)
    hidden = draw_hidden(jax.random.fold_in(arg_keys[4], 71), 0)
    table = draw_table(jax.random.fold_in(arg_keys[4], 71), 0)
    subset_ids = draw_subset_ids(jax.random.fold_in(arg_keys[4], 71), 0)
    targets = draw_targets(jax.random.fold_in(arg_keys[4], 71), 0)
    return dict(hidden=hidden, table=table, subset_ids=subset_ids, targets=targets)


LOSS_SCALE = 32.0


def reference(hidden, table, subset_ids, targets):
    head_rows = table[subset_ids]
    logits = jnp.dot(hidden, head_rows.T, preferred_element_type=jnp.float32)
    row_peak = jnp.max(logits, axis=1, keepdims=True)
    shifted = jnp.exp(logits - row_peak)
    row_total = jnp.sum(shifted, axis=1, keepdims=True)
    softmax_probs = shifted / row_total
    target = targets.astype(jnp.float32)
    row_mass = jnp.sum(target, axis=1, keepdims=True)
    logit_grad = (LOSS_SCALE * (softmax_probs * row_mass - target)).astype(jnp.bfloat16)
    row_grad = jnp.dot(logit_grad.T, hidden, preferred_element_type=jnp.float32).astype(jnp.bfloat16)
    table_grad = jnp.zeros(table.shape, jnp.bfloat16).at[subset_ids].set(row_grad)
    hidden_grad = jnp.dot(logit_grad, head_rows, preferred_element_type=jnp.float32).astype(jnp.bfloat16)
    return logits.astype(jnp.bfloat16), hidden_grad, table_grad
```

```python
import jax
import jax.numpy as jnp
from jax import lax
from jax.sharding import Mesh, PartitionSpec as P

LOSS_SCALE = 32.0
LOW = 64
FAR = -3.0e38
ROWS = ("x", "core")
VOCAB = ("y", "z")
f32, bf16, i32, i16 = jnp.float32, jnp.bfloat16, jnp.int32, jnp.int16


def shift(axis, by):
    n = lax.axis_size(axis)
    return [(i, (i + by) % n) for i in range(n)]


def matmul(a, b, ca, cb, dtype=f32):
    return lax.dot_general(a, b, (((ca,), (cb,)), ((), ())), preferred_element_type=dtype)


def at(blocks, index):
    return lax.dynamic_index_in_dim(blocks, index, 0, keepdims=False)


def encode(part):
    top = jnp.maximum(jnp.max(jnp.abs(part), axis=-1, keepdims=True), 1e-30)
    return jnp.round(part * (32767.0 / top)).astype(i16), top * (1.0 / 32767.0)


def slots_of(subset_ids, owner_rows, vocab_count, capacity):
    count = subset_ids.shape[0]
    owner_of = subset_ids // owner_rows
    onehot = (owner_of[:, None] == jnp.arange(vocab_count)[None, :]).astype(bf16)
    earlier = (jnp.arange(count)[:, None] > jnp.arange(count)[None, :]).astype(bf16)
    before = matmul(earlier, onehot, 1, 0)
    rank = jnp.sum(before * onehot.astype(f32), axis=1).astype(i32)
    return owner_of * capacity + rank, subset_ids % owner_rows


def on_device(hidden, table, subset_ids, targets):
    nx, nc, ny, nz = (lax.axis_size(a) for a in ("x", "core", "y", "z"))
    x, core, y, z = (lax.axis_index(a) for a in ("x", "core", "y", "z"))
    vocab_count = ny * nz
    positions, width = hidden.shape
    owner_rows = table.shape[0]
    sub_dev = subset_ids.shape[0]
    pos_dev = targets.shape[0]
    capacity = 2 * sub_dev // vocab_count
    slots = vocab_count * capacity

    own_hidden = hidden.reshape(nx, nc, pos_dev, width)
    swap = [(0, 1), (1, 0)]
    table_far = lax.ppermute(table, "core", swap)
    mine = lax.dynamic_index_in_dim(own_hidden, core, 1, keepdims=False)
    hidden_far = lax.ppermute(
        lax.dynamic_index_in_dim(own_hidden, 1 - core, 1, keepdims=False), "core", swap
    )

    slot_index, local_row = slots_of(subset_ids, owner_rows, vocab_count, capacity)
    to_slot = (jnp.arange(slots)[:, None] == slot_index[None, :]).astype(bf16)
    side = jnp.stack([local_row // LOW, local_row % LOW, jnp.ones_like(local_row)]).astype(bf16)
    pad = (-(pos_dev + side.shape[0])) % 128
    sent = jnp.concatenate([targets, side, jnp.zeros((pad, sub_dev), bf16)], axis=0)
    payload = matmul(to_slot, sent, 1, 1, bf16)
    got = lax.all_to_all(
        payload.reshape(vocab_count, capacity, -1), VOCAB, split_axis=0, concat_axis=0, tiled=True
    ).reshape(slots, -1)
    info = got[:, pos_dev : pos_dev + 3].astype(i32)
    row_of = jnp.where(info[:, 2] > 0, info[:, 0] * LOW + info[:, 1], -1)
    to_row = (row_of[:, None] == jnp.arange(owner_rows)[None, :]).astype(bf16)
    landed = matmul(got, to_row, 0, 0)
    target = landed[:pos_dev]
    chosen = landed[pos_dev + 2 : pos_dev + 3] > 0.5

    total = None
    arrived = []
    for k in (2, 1, 3, 0):
        to = (x + k) % nx
        part = matmul(at(mine, to), table, 1, 1) + matmul(at(hidden_far, to), table_far, 1, 1)
        if k == 0:
            total = part
            continue
        code, step = encode(part)
        arrived.append(
            (lax.ppermute(code, "x", shift("x", k)), lax.ppermute(step, "x", shift("x", k)))
        )
    logits = total
    for code, step in arrived:
        logits = logits + code.astype(f32) * step

    peak = jnp.max(jnp.where(chosen, logits, FAR), axis=1)
    part_total = jnp.sum(jnp.where(chosen, jnp.exp(logits - peak[:, None]), 0.0), axis=1)
    mass = jnp.sum(target, axis=1)
    stats = jnp.stack([peak, part_total, mass])
    stats = jnp.broadcast_to(stats[None], (vocab_count,) + stats.shape)
    stats = lax.all_to_all(stats, VOCAB, split_axis=0, concat_axis=0, tiled=True)
    row_peak = jnp.max(stats[:, 0], axis=0)
    row_total = jnp.sum(stats[:, 1] * jnp.exp(stats[:, 0] - row_peak[None, :]), axis=0)
    row_mass = jnp.sum(stats[:, 2], axis=0)
    probs = jnp.exp(logits - row_peak[:, None]) / row_total[:, None]
    grad = jnp.where(chosen, LOSS_SCALE * (probs * row_mass[:, None] - target), 0.0).astype(bf16)

    blocks = [grad] + [lax.ppermute(grad, "x", shift("x", -j)) for j in range(1, nx)]
    own = jnp.stack(blocks)
    other = lax.ppermute(own, "core", swap)
    first = jnp.where(core == 0, own, other)
    second = jnp.where(core == 0, other, own)
    grad_all = jnp.stack([first, second], axis=1)
    turned = jnp.stack([at(own_hidden, (x + j) % nx) for j in range(nx)])
    flat = grad_all.reshape(positions, owner_rows)
    table_grad = matmul(flat, turned.reshape(positions, width), 0, 0).astype(bf16)

    hidden_part = matmul(flat, table, 1, 0).reshape(nx, nc * pos_dev, width)
    mine_y = at(hidden_part, (y - x) % nx)
    for k in (2, 1, 3):
        code, step = encode(at(hidden_part, (y + k - x) % nx))
        code, step = (lax.ppermute(a, "y", shift("y", k)) for a in (code, step))
        mine_y = mine_y + code.astype(f32) * step
    out_pos = positions // vocab_count
    code, step = encode(mine_y.reshape(nz, out_pos, width))
    code, step = (
        lax.all_to_all(a, "z", split_axis=0, concat_axis=0, tiled=True) for a in (code, step)
    )
    hidden_grad = jnp.sum(code.astype(f32) * step, axis=0).astype(bf16)

    out = matmul(to_row, logits.astype(bf16), 1, 1, bf16)
    out = lax.all_to_all(
        out.reshape(vocab_count, capacity, pos_dev), VOCAB, split_axis=0, concat_axis=0, tiled=True
    ).reshape(slots, pos_dev)
    draft = matmul(out, to_slot, 0, 0, bf16)
    return draft, hidden_grad, table_grad


def solution(mesh):
    fine = Mesh(mesh.devices.reshape(4, 2, 4, 8), ROWS + VOCAB)
    return jax.shard_map(
        on_device,
        mesh=fine,
        in_specs=(P(None, ROWS), P(VOCAB, ROWS), P(VOCAB), P(ROWS, VOCAB)),
        out_specs=(P(ROWS, VOCAB), P(VOCAB, ROWS), P(VOCAB, ROWS)),
        check_vma=False,
    )
```

```python
import functools

import jax
import jax.numpy as jnp
from jax import lax
from jax.experimental import pallas as pl
from jax.experimental.pallas import tpu as pltpu
from jax.sharding import Mesh, PartitionSpec as P

LOSS_SCALE = 32.0
LOW = 64
FAR = -3.0e38
SIDE = 128
CHUNKS = 3
ROWS = ("x", "core")
VOCAB = ("y", "z")
VMEM = 56 * 1024 * 1024
f32, bf16, i32, i16 = jnp.float32, jnp.bfloat16, jnp.int32, jnp.int16
SWAP = [(0, 1), (1, 0)]


def shift(axis, by):
    n = lax.axis_size(axis)
    return [(i, (i + by) % n) for i in range(n)]


def matmul(a, b, ca, cb, dtype=f32):
    return lax.dot_general(a, b, (((ca,), (cb,)), ((), ())), preferred_element_type=dtype)


def store_code(part, put):
    top = jnp.maximum(jnp.max(jnp.abs(part), axis=1, keepdims=True), 1e-30)
    power = jnp.ceil(jnp.log(top) * 1.4426950408889634) - 15.0
    code = jnp.round(part * jnp.exp2(-power))
    code = jnp.minimum(jnp.maximum(code, -32767.0), 32767.0)
    width = part.shape[1]
    put(slice(0, width), code.astype(i32).astype(i16))
    side = jnp.broadcast_to(power, (part.shape[0], SIDE))
    put(slice(width, width + SIDE), side.astype(i32).astype(i16))


def decode(code):
    width = code.shape[-1] - SIDE
    return code[..., :width].astype(f32) * jnp.exp2(code[..., width : width + 1].astype(f32))


def logits_kernel(nx, tile, pos, near, far, table, table_far, code, own, part):
    step = pl.program_id(0)
    rows = near.shape[2]
    width = near.shape[3]
    columns = pl.ds(pl.multiple_of(step * tile, tile), tile)
    left = near[...].reshape(nx * rows, width)
    right = far[...].reshape(nx * rows, width)
    out = matmul(left, table[...], 1, 1) + matmul(right, table_far[...], 1, 1)
    part[:, :, columns] = out.reshape(nx, rows, tile)

    @pl.when(step == pl.num_programs(0) - 1)
    def _():
        x = pos[0]
        for k in range(1, nx):
            to = lax.rem(x + k, nx)

            def body(r, _, to=to, k=k):
                span = pl.ds(pl.multiple_of(r * 16, 16), 16)

                def put(cols, value):
                    code[k - 1, span, cols] = value

                store_code(part[to, span, :], put)
                return 0

            lax.fori_loop(0, rows // 16, body, 0)
        own[...] = part[x]


def partial_logits(pos, near, far, table, table_far):
    nx, nc, rows, width = near.shape
    owner_rows = table.shape[0]
    tile = owner_rows // 4
    return pl.pallas_call(
        functools.partial(logits_kernel, nx, tile),
        grid_spec=pltpu.PrefetchScalarGridSpec(
            num_scalar_prefetch=1,
            grid=(owner_rows // tile,),
            in_specs=[
                pl.BlockSpec((nx, 1, rows, width), lambda t, pos: (0, pos[1], 0, 0)),
                pl.BlockSpec((nx, rows, width), lambda t, pos: (0, 0, 0)),
                pl.BlockSpec((tile, width), lambda t, pos: (t, 0)),
                pl.BlockSpec((tile, width), lambda t, pos: (t, 0)),
            ],
            out_specs=[
                pl.BlockSpec((nx - 1, rows, owner_rows + SIDE), lambda t, pos: (0, 0, 0)),
                pl.BlockSpec((rows, owner_rows), lambda t, pos: (0, 0)),
            ],
            scratch_shapes=[pltpu.VMEM((nx, rows, owner_rows), f32)],
        ),
        out_shape=[
            jax.ShapeDtypeStruct((nx - 1, rows, owner_rows + SIDE), i16),
            jax.ShapeDtypeStruct((rows, owner_rows), f32),
        ],
        compiler_params=pltpu.CompilerParams(vmem_limit_bytes=VMEM),
        cost_estimate=pl.CostEstimate(
            flops=4 * nx * rows * width * owner_rows, bytes_accessed=16 << 20, transcendentals=0
        ),
    )(pos, near, far, table, table_far)


def hidden_kernel(nx, nc, tile, pos, *refs):
    blocks, (table, _, code, own, grads, part) = refs[: nx * nc], refs[nx * nc :]
    step = pl.program_id(0)
    x, core, y = pos[0], pos[1], pos[2]
    rows, owner_rows = blocks[0].shape

    @pl.when(step == 0)
    def _():
        for j in range(nx):
            to = lax.rem(x + j, nx)
            grads[0, to, core] = blocks[j][...]
            grads[0, to, 1 - core] = blocks[nx + j][...]

    columns = pl.ds(pl.multiple_of(step * tile, tile), tile)
    left = grads[...].reshape(nx * nc * rows, owner_rows)
    out = matmul(left, table[...], 1, 0)
    part[:, :, columns] = out.reshape(nx, nc * rows, tile)

    @pl.when(step == pl.num_programs(0) - 1)
    def _():
        for k in range(1, nx):
            to = lax.rem(y + k, nx)

            def body(r, _, to=to, k=k):
                span = pl.ds(pl.multiple_of(r * 16, 16), 16)

                def put(cols, value):
                    code[k - 1, span, cols] = value

                store_code(part[to, span, :], put)
                return 0

            lax.fori_loop(0, nc * rows // 16, body, 0)
        own[...] = part[y]


def hidden_parts(pos, blocks, table, grads, chunk, nx, nc):
    rows, owner_rows = blocks[0].shape
    width = table.shape[1]
    tile = width // 4
    count = len(blocks)
    return pl.pallas_call(
        functools.partial(hidden_kernel, nx, nc, tile),
        grid_spec=pltpu.PrefetchScalarGridSpec(
            num_scalar_prefetch=1,
            grid=(width // tile,),
            in_specs=[pl.BlockSpec((rows, owner_rows), lambda t, pos: (0, 0))] * count
            + [
                pl.BlockSpec((owner_rows, tile), lambda t, pos: (0, t)),
                pl.BlockSpec(memory_space=pl.ANY),
            ],
            out_specs=[
                pl.BlockSpec((nx - 1, nc * rows, width + SIDE), lambda t, pos: (0, 0, 0)),
                pl.BlockSpec((nc * rows, width), lambda t, pos: (0, 0)),
                pl.BlockSpec(
                    (1, nx, nc, rows, owner_rows), lambda t, pos: (chunk, 0, 0, 0, 0)
                ),
            ],
            scratch_shapes=[pltpu.VMEM((nx, nc * rows, width), f32)],
        ),
        out_shape=[
            jax.ShapeDtypeStruct((nx - 1, nc * rows, width + SIDE), i16),
            jax.ShapeDtypeStruct((nc * rows, width), f32),
            jax.ShapeDtypeStruct(grads.shape, grads.dtype),
        ],
        input_output_aliases={count + 2: 2},
        compiler_params=pltpu.CompilerParams(vmem_limit_bytes=VMEM),
        cost_estimate=pl.CostEstimate(
            flops=2 * nx * nc * rows * width * owner_rows,
            bytes_accessed=8 << 20,
            transcendentals=0,
        ),
    )(pos, *blocks, table, grads)


def add_kernel(own, a, b, c, code):
    rows = code.shape[1]

    def body(r, _):
        span = pl.ds(pl.multiple_of(r * rows, rows), rows)
        total = own[span, :]
        for ref in (a, b, c):
            total = total + decode(ref[span, :])

        def put(cols, value):
            code[r, :, cols] = value

        store_code(total, put)
        return 0

    lax.fori_loop(0, code.shape[0], body, 0)


def add_and_code(own, arrived, pieces):
    rows, width = own.shape
    return pl.pallas_call(
        add_kernel,
        out_shape=jax.ShapeDtypeStruct((pieces, rows // pieces, width + SIDE), i16),
        compiler_params=pltpu.CompilerParams(vmem_limit_bytes=VMEM),
    )(own, *arrived)


def slots_of(subset_ids, owner_rows, vocab_count, capacity):
    count = subset_ids.shape[0]
    owner_of = subset_ids // owner_rows
    onehot = (owner_of[:, None] == jnp.arange(vocab_count)[None, :]).astype(bf16)
    earlier = (jnp.arange(count)[:, None] > jnp.arange(count)[None, :]).astype(bf16)
    before = matmul(earlier, onehot, 1, 0)
    rank = jnp.sum(before * onehot.astype(f32), axis=1).astype(i32)
    return owner_of * capacity + rank, subset_ids % owner_rows


def on_device(hidden, table, subset_ids, targets):
    nx, nc, ny, nz = (lax.axis_size(a) for a in ("x", "core", "y", "z"))
    x, core, y = (lax.axis_index(a) for a in ("x", "core", "y"))
    pos = jnp.stack([x, core, y]).astype(i32)
    vocab_count = ny * nz
    positions, width = hidden.shape
    owner_rows = table.shape[0]
    sub_dev = subset_ids.shape[0]
    pos_dev = targets.shape[0]
    capacity = 2 * sub_dev // vocab_count
    slots = vocab_count * capacity
    out_pos = positions // vocab_count
    small = out_pos // CHUNKS

    near = hidden.reshape(nx, nc, pos_dev, width)
    table_far = lax.ppermute(table, "core", SWAP)
    far = lax.ppermute(
        lax.dynamic_index_in_dim(near, 1 - core, 1, keepdims=False), "core", SWAP
    )

    slot_index, local_row = slots_of(subset_ids, owner_rows, vocab_count, capacity)
    to_slot = (jnp.arange(slots)[:, None] == slot_index[None, :]).astype(bf16)
    side = jnp.stack([local_row // LOW, local_row % LOW, jnp.ones_like(local_row)]).astype(bf16)
    pad = (-(pos_dev + side.shape[0])) % 128
    sent = jnp.concatenate([targets, side, jnp.zeros((pad, sub_dev), bf16)], axis=0)
    payload = matmul(to_slot, sent, 1, 1, bf16)

    code, own = partial_logits(pos, near, far, table, table_far)
    code, own, payload = lax.optimization_barrier((code, own, payload))
    arrived = [lax.ppermute(code[k - 1], "x", shift("x", k)) for k in (2, 1, 3)]

    got = lax.all_to_all(
        payload.reshape(vocab_count, capacity, -1), VOCAB, split_axis=0, concat_axis=0, tiled=True
    ).reshape(slots, -1)
    info = got[:, pos_dev : pos_dev + 3].astype(i32)
    row_of = jnp.where(info[:, 2] > 0, info[:, 0] * LOW + info[:, 1], -1)
    to_row = (row_of[:, None] == jnp.arange(owner_rows)[None, :]).astype(bf16)
    landed = matmul(got, to_row, 0, 0)
    target = landed[:pos_dev]
    chosen = landed[pos_dev + 2 : pos_dev + 3] > 0.5

    logits = own
    for block in arrived:
        logits = logits + decode(block)

    peak = jnp.max(jnp.where(chosen, logits, FAR), axis=1)
    part_total = jnp.sum(jnp.where(chosen, jnp.exp(logits - peak[:, None]), 0.0), axis=1)
    mass = jnp.sum(target, axis=1)
    stats = jnp.stack([peak, part_total, mass])
    stats = jnp.broadcast_to(stats[None], (vocab_count,) + stats.shape)
    stats = lax.all_to_all(stats, VOCAB, split_axis=0, concat_axis=0, tiled=True)
    row_peak = jnp.max(stats[:, 0], axis=0)
    row_total = jnp.sum(stats[:, 1] * jnp.exp(stats[:, 0] - row_peak[None, :]), axis=0)
    row_mass = jnp.sum(stats[:, 2], axis=0)
    probs = jnp.exp(logits - row_peak[:, None]) / row_total[:, None]
    grad = jnp.where(chosen, LOSS_SCALE * (probs * row_mass[:, None] - target), 0.0).astype(bf16)
    grad = grad.reshape(pos_dev // out_pos, CHUNKS, small, owner_rows)

    grads = jnp.zeros((CHUNKS, nx, nc, pos_dev // CHUNKS, owner_rows), bf16)
    pieces = []
    before = []
    for c in range(CHUNKS):
        mine = grad[:, c].reshape(pos_dev // CHUNKS, owner_rows)
        if before:
            mine, *before = lax.optimization_barrier((mine, *before))
        blocks = [mine] + [lax.ppermute(mine, "x", shift("x", -j)) for j in range(1, nx)]
        before = blocks[1:]
        blocks = blocks + [lax.ppermute(b, "core", SWAP) for b in blocks]
        code, own, grads = hidden_parts(pos, blocks, table, grads, c, nx, nc)
        arrived = [lax.ppermute(code[k - 1], "y", shift("y", k)) for k in (2, 1, 3)]
        code = add_and_code(own, arrived, nz)
        code = lax.all_to_all(code, "z", split_axis=0, concat_axis=0, tiled=True)
        pieces.append(jnp.sum(decode(code), axis=0).astype(bf16))
    hidden_grad = jnp.concatenate(pieces, axis=0)

    ordered = hidden.reshape(nx, nc, pos_dev // out_pos, CHUNKS, small, width)
    ordered = ordered.transpose(3, 0, 1, 2, 4, 5).reshape(positions, width)
    table_grad = matmul(grads.reshape(positions, owner_rows), ordered, 0, 0).astype(bf16)

    out = matmul(to_row, logits.astype(bf16), 1, 1, bf16)
    out = lax.all_to_all(
        out.reshape(vocab_count, capacity, pos_dev), VOCAB, split_axis=0, concat_axis=0, tiled=True
    ).reshape(slots, pos_dev)
    draft = matmul(out, to_slot, 0, 0, bf16)
    return draft, hidden_grad, table_grad


def solution(mesh):
    fine = Mesh(mesh.devices.reshape(4, 2, 4, 8), ROWS + VOCAB)
    return jax.shard_map(
        on_device,
        mesh=fine,
        in_specs=(P(None, ROWS), P(VOCAB, ROWS), P(VOCAB), P(ROWS, VOCAB)),
        out_specs=(P(ROWS, VOCAB), P(VOCAB, ROWS), P(VOCAB, ROWS)),
        check_vma=False,
    )
```

```python
import functools

import jax
import jax.numpy as jnp
from jax import lax
from jax.experimental import pallas as pl
from jax.experimental.pallas import tpu as pltpu
from jax.sharding import Mesh, PartitionSpec as P

LOSS_SCALE = 32.0
LOW = 64
GROUP = 96
TILES = 4
HTILES = 4
FAR = -3.0e38
SIDE = 128
CHUNKS = 2
ROWS = ("x", "core")
VOCAB = ("y", "z")
VMEM = 56 * 1024 * 1024
f32, bf16, i32, i16 = jnp.float32, jnp.bfloat16, jnp.int32, jnp.int16
SWAP = [(0, 1), (1, 0)]


def shift(axis, by):
    n = lax.axis_size(axis)
    return [(i, (i + by) % n) for i in range(n)]


def matmul(a, b, ca, cb, dtype=f32):
    return lax.dot_general(a, b, (((ca,), (cb,)), ((), ())), preferred_element_type=dtype)


def store_code(part, put):
    top = jnp.maximum(jnp.max(jnp.abs(part), axis=1, keepdims=True), 1e-30) * 1.0001
    power = jnp.ceil(jnp.log(top) * 1.4426950408889634) - 15.0
    code = jnp.round(part * jnp.exp2(-power)).astype(i32).astype(i16)
    width = part.shape[1]
    put(slice(0, width), code)
    side = jnp.broadcast_to(power, (part.shape[0], SIDE))
    put(slice(width, width + SIDE), side.astype(i32).astype(i16))


def decode(code):
    width = code.shape[-1] - SIDE
    return code[..., :width].astype(f32) * jnp.exp2(code[..., width : width + 1].astype(f32))


def code_rows(source, target):
    def body(r, _):
        span = pl.ds(pl.multiple_of(r * GROUP, GROUP), GROUP)

        def put(cols, value):
            target[span, cols] = value

        store_code(source(span), put)
        return 0

    lax.fori_loop(0, target.shape[0] // GROUP, body, 0)


def logits_kernel(nx, tile, pos, near, far, table, table_far, *refs):
    codes, (own, part) = refs[:-2], refs[-2:]
    step = pl.program_id(0)
    rows, width = near.shape[3:]
    columns = pl.ds(pl.multiple_of(step * tile, tile), tile)
    left = near[...].reshape(nx * rows, width)
    right = far[...].reshape(nx * rows, width)
    out = matmul(left, table[...], 1, 1) + matmul(right, table_far[...], 1, 1)
    part[:, :, columns] = out.reshape(nx, rows, tile)

    @pl.when(step == pl.num_programs(0) - 1)
    def _():
        x = pos[0]
        for k, code in enumerate(codes, 1):
            to = lax.rem(x + k, nx)
            code_rows(lambda span, to=to: part[to, span, :], code)
        own[...] = part[x]


def partial_logits(pos, near, far, table, table_far, chunk):
    _, nx, nc, rows, width = near.shape
    owner_rows = table.shape[0]
    tile = owner_rows // TILES
    return pl.pallas_call(
        functools.partial(logits_kernel, nx, tile),
        grid_spec=pltpu.PrefetchScalarGridSpec(
            num_scalar_prefetch=1,
            grid=(owner_rows // tile,),
            in_specs=[
                pl.BlockSpec((1, nx, 1, rows, width), lambda t, pos: (chunk, 0, pos[1], 0, 0)),
                pl.BlockSpec((1, nx, rows, width), lambda t, pos: (chunk, 0, 0, 0)),
                pl.BlockSpec((tile, width), lambda t, pos: (t, 0)),
                pl.BlockSpec((tile, width), lambda t, pos: (t, 0)),
            ],
            out_specs=[pl.BlockSpec((rows, owner_rows + SIDE), lambda t, pos: (0, 0))] * (nx - 1)
            + [pl.BlockSpec((rows, owner_rows), lambda t, pos: (0, 0))],
            scratch_shapes=[pltpu.VMEM((nx, rows, owner_rows), f32)],
        ),
        out_shape=[jax.ShapeDtypeStruct((rows, owner_rows + SIDE), i16)] * (nx - 1)
        + [jax.ShapeDtypeStruct((rows, owner_rows), f32)],
        compiler_params=pltpu.CompilerParams(vmem_limit_bytes=VMEM),
        cost_estimate=pl.CostEstimate(
            flops=4 * nx * rows * width * owner_rows, bytes_accessed=16 << 20, transcendentals=0
        ),
    )(pos, near, far, table, table_far)


def hidden_kernel(nx, nc, tile, pos, *refs):
    blocks, table, rest = refs[: nx * nc], refs[nx * nc], refs[-(nx + 2) :]
    codes, (own, grads, part) = rest[: nx - 1], rest[nx - 1 :]
    step = pl.program_id(0)
    x, core, y = pos[0], pos[1], pos[2]
    rows, owner_rows = blocks[0].shape

    @pl.when(step == 0)
    def _():
        for j in range(nx):
            to = lax.rem(x + j, nx)
            grads[0, to, core] = blocks[j][...]
            grads[0, to, 1 - core] = blocks[nx + j][...]

    columns = pl.ds(pl.multiple_of(step * tile, tile), tile)
    left = grads[...].reshape(nx * nc * rows, owner_rows)
    out = matmul(left, table[...], 1, 0)
    part[:, :, columns] = out.reshape(nx, nc * rows, tile)

    @pl.when(step == pl.num_programs(0) - 1)
    def _():
        for k, code in enumerate(codes, 1):
            to = lax.rem(y + k, nx)
            code_rows(lambda span, to=to: part[to, span, :], code)
        own[...] = part[y]


def hidden_parts(pos, blocks, table, grads, chunk, nx, nc):
    rows, owner_rows = blocks[0].shape
    width = table.shape[1]
    tile = width // HTILES
    count = len(blocks)
    every = jax.ShapeDtypeStruct((CHUNKS, nx, nc, rows, owner_rows), bf16)
    held = [] if grads is None else [grads]
    return pl.pallas_call(
        functools.partial(hidden_kernel, nx, nc, tile),
        grid_spec=pltpu.PrefetchScalarGridSpec(
            num_scalar_prefetch=1,
            grid=(width // tile,),
            in_specs=[pl.BlockSpec((rows, owner_rows), lambda t, pos: (0, 0))] * count
            + [pl.BlockSpec((owner_rows, tile), lambda t, pos: (0, t))]
            + [pl.BlockSpec(memory_space=pl.ANY)] * len(held),
            out_specs=[pl.BlockSpec((nc * rows, width + SIDE), lambda t, pos: (0, 0))] * (nx - 1)
            + [
                pl.BlockSpec((nc * rows, width), lambda t, pos: (0, 0)),
                pl.BlockSpec(
                    (1, nx, nc, rows, owner_rows), lambda t, pos: (chunk, 0, 0, 0, 0)
                ),
            ],
            scratch_shapes=[pltpu.VMEM((nx, nc * rows, width), f32)],
        ),
        out_shape=[jax.ShapeDtypeStruct((nc * rows, width + SIDE), i16)] * (nx - 1)
        + [jax.ShapeDtypeStruct((nc * rows, width), f32), every],
        input_output_aliases={count + 2: nx} if held else {},
        compiler_params=pltpu.CompilerParams(vmem_limit_bytes=VMEM),
        cost_estimate=pl.CostEstimate(
            flops=2 * nx * nc * rows * width * owner_rows,
            bytes_accessed=8 << 20,
            transcendentals=0,
        ),
    )(pos, *blocks, table, *held)


def add_kernel(own, a, b, c, *rest):
    code = rest[-1]
    part = own[...]
    for ref in (a, b, c):
        part = part + decode(ref[...])

    def put(cols, value):
        code[:, :, cols] = value.reshape(code.shape[0], code.shape[1], -1)

    store_code(part, put)


def add_and_code(own, arrived, pieces, after=()):
    rows, width = own.shape
    whole = pl.BlockSpec(memory_space=pltpu.VMEM)
    return pl.pallas_call(
        add_kernel,
        in_specs=[whole] * 4 + [pl.BlockSpec(memory_space=pl.ANY)] * len(after),
        out_specs=whole,
        out_shape=jax.ShapeDtypeStruct((pieces, rows // pieces, width + SIDE), i16),
        compiler_params=pltpu.CompilerParams(vmem_limit_bytes=VMEM),
    )(own, *arrived, *after)


def slots_of(subset_ids, owner_rows, vocab_count, capacity):
    count = subset_ids.shape[0]
    owner_of = subset_ids // owner_rows
    onehot = (owner_of[:, None] == jnp.arange(vocab_count)[None, :]).astype(bf16)
    earlier = (jnp.arange(count)[:, None] > jnp.arange(count)[None, :]).astype(bf16)
    before = matmul(earlier, onehot, 1, 0)
    rank = jnp.sum(before * onehot.astype(f32), axis=1).astype(i32)
    return owner_of * capacity + rank, subset_ids % owner_rows


def on_device(hidden, table, subset_ids, targets):
    nx, nc, ny, nz = (lax.axis_size(a) for a in ("x", "core", "y", "z"))
    x, core, y = (lax.axis_index(a) for a in ("x", "core", "y"))
    pos = jnp.stack([x, core, y]).astype(i32)
    vocab_count = ny * nz
    positions, width = hidden.shape
    owner_rows = table.shape[0]
    sub_dev = subset_ids.shape[0]
    pos_dev = targets.shape[0]
    capacity = 2 * sub_dev // vocab_count
    slots = vocab_count * capacity
    out_pos = positions // vocab_count
    small = out_pos // CHUNKS
    rows = pos_dev // CHUNKS

    table_far = lax.ppermute(table, "core", SWAP)
    ordered = hidden.reshape(nx, nc, pos_dev // out_pos, CHUNKS, small, width)
    ordered = ordered.transpose(3, 0, 1, 2, 4, 5).reshape(CHUNKS, nx, nc, rows, width)
    far = lax.dynamic_index_in_dim(ordered, 1 - core, 2, keepdims=False)
    far = lax.ppermute(far, "core", SWAP)

    targets = targets.reshape(pos_dev // out_pos, CHUNKS, small, sub_dev)
    targets = targets.transpose(1, 0, 2, 3).reshape(pos_dev, sub_dev)
    slot_index, local_row = slots_of(subset_ids, owner_rows, vocab_count, capacity)
    to_slot = (jnp.arange(slots)[:, None] == slot_index[None, :]).astype(bf16)
    side = jnp.stack([local_row // LOW, local_row % LOW, jnp.ones_like(local_row)]).astype(bf16)
    pad = (-(pos_dev + side.shape[0])) % 128
    sent = jnp.concatenate([targets, side, jnp.zeros((pad, sub_dev), bf16)], axis=0)
    payload = matmul(to_slot, sent, 1, 1, bf16)
    payload, far = lax.optimization_barrier((payload, far))
    got = lax.all_to_all(
        payload.reshape(vocab_count, capacity, -1), VOCAB, split_axis=0, concat_axis=0, tiled=True
    ).reshape(slots, -1)

    parts = []
    for c in range(CHUNKS):
        *codes, own = partial_logits(pos, ordered, far, table, table_far, c)
        parts.append(
            [own] + [lax.ppermute(codes[k - 1], "x", shift("x", k)) for k in (2, 1, 3)]
        )

    got, *parts[0] = lax.optimization_barrier((got, *parts[0], parts[1][0]))[:-1]
    info = got[:, pos_dev : pos_dev + 3].astype(i32)
    row_of = jnp.where(info[:, 2] > 0, info[:, 0] * LOW + info[:, 1], -1)
    to_row = (row_of[:, None] == jnp.arange(owner_rows)[None, :]).astype(bf16)
    landed = matmul(got, to_row, 0, 0)
    chosen = landed[pos_dev + 2 : pos_dev + 3] > 0.5

    logits, local = [], []
    for c in range(CHUNKS):
        if c:
            *parts[c], local[-1] = lax.optimization_barrier((*parts[c], local[-1]))
        here = parts[c][0]
        for block in parts[c][1:]:
            here = here + decode(block)
        peak = jnp.max(jnp.where(chosen, here, FAR), axis=1)
        total = jnp.sum(jnp.where(chosen, jnp.exp(here - peak[:, None]), 0.0), axis=1)
        logits.append(here)
        local.append(jnp.stack([peak, total, jnp.sum(landed[c * rows : (c + 1) * rows], axis=1)]))
    stats = jnp.stack(local).reshape(1, CHUNKS * 3 * rows)
    stats = jnp.broadcast_to(stats, (vocab_count,) + stats.shape[1:])
    stats = lax.all_to_all(stats, VOCAB, split_axis=0, concat_axis=0, tiled=True)
    stats = stats.reshape(vocab_count, CHUNKS, 3, rows)
    row_peak = jnp.max(stats[:, :, 0], axis=0)
    row_total = jnp.sum(stats[:, :, 1] * jnp.exp(stats[:, :, 0] - row_peak[None]), axis=0)
    row_mass = jnp.sum(stats[:, :, 2], axis=0)
    mine = []
    for c in range(CHUNKS):
        if c:
            row_peak, *_ = lax.optimization_barrier((row_peak, *mine))
        probs = jnp.exp(logits[c] - row_peak[c][:, None]) / row_total[c][:, None]
        grad = LOSS_SCALE * (probs * row_mass[c][:, None] - landed[c * rows : (c + 1) * rows])
        mine.append(jnp.where(chosen, grad, 0.0).astype(bf16))

    grads = None
    pieces = []
    before = []
    for c in range(CHUNKS):
        if before:
            mine[c], *before = lax.optimization_barrier((mine[c], *before))
        blocks = [mine[c]] + [lax.ppermute(mine[c], "x", shift("x", -j)) for j in range(1, nx)]
        before = blocks[1:]
        blocks = blocks + [lax.ppermute(b, "core", SWAP) for b in blocks]
        *codes, own, grads = hidden_parts(pos, blocks, table, grads, c, nx, nc)
        arrived = [lax.ppermute(codes[k - 1], "y", shift("y", k)) for k in (2, 1, 3)]
        after = ()
        if c == CHUNKS - 1:
            table_grad = matmul(
                grads.reshape(positions, owner_rows), ordered.reshape(positions, width), 0, 0
            ).astype(bf16)
            after = (table_grad,)
        code = add_and_code(own, arrived, nz, after)
        code = lax.all_to_all(code, "z", split_axis=0, concat_axis=0, tiled=True)
        pieces.append(jnp.sum(decode(code), axis=0).astype(bf16))
    hidden_grad = jnp.concatenate(pieces, axis=0)

    out = matmul(to_row, jnp.concatenate(logits, axis=0).astype(bf16), 1, 1, bf16)
    out = lax.all_to_all(
        out.reshape(vocab_count, capacity, pos_dev), VOCAB, split_axis=0, concat_axis=0, tiled=True
    ).reshape(slots, pos_dev)
    draft = matmul(out, to_slot, 0, 0, bf16)
    draft = draft.reshape(CHUNKS, pos_dev // out_pos, small, sub_dev).transpose(1, 0, 2, 3)
    return draft.reshape(pos_dev, sub_dev), hidden_grad, table_grad


def solution(mesh):
    fine = Mesh(mesh.devices.reshape(4, 2, 4, 8), ROWS + VOCAB)
    return jax.shard_map(
        on_device,
        mesh=fine,
        in_specs=(P(None, ROWS), P(VOCAB, ROWS), P(VOCAB), P(ROWS, VOCAB)),
        out_specs=(P(ROWS, VOCAB), P(VOCAB, ROWS), P(VOCAB, ROWS)),
        check_vma=False,
    )
```

```python
import functools

import jax
import jax.numpy as jnp
from jax import lax
from jax.experimental import pallas as pl
from jax.experimental.pallas import tpu as pltpu
from jax.sharding import Mesh, PartitionSpec as P

LOSS_SCALE = 32.0
LOW = 64
GROUP = 96
TILES = 4
HTILES = 4
FAR = -3.0e38
SIDE = 128
CHUNKS = 2
ROWS = ("x", "core")
VOCAB = ("y", "z")
VMEM = 24 * 1024 * 1024
f32, bf16, i32, i16 = jnp.float32, jnp.bfloat16, jnp.int32, jnp.int16
SWAP = [(0, 1), (1, 0)]


def shift(axis, by):
    n = lax.axis_size(axis)
    return [(i, (i + by) % n) for i in range(n)]


def matmul(a, b, ca, cb, dtype=f32):
    return lax.dot_general(a, b, (((ca,), (cb,)), ((), ())), preferred_element_type=dtype)


def store_code(part, put):
    top = jnp.maximum(jnp.max(jnp.abs(part), axis=1, keepdims=True), 1e-30) * 1.0001
    power = jnp.ceil(jnp.log(top) * 1.4426950408889634) - 15.0
    code = jnp.round(part * jnp.exp2(-power)).astype(i32).astype(i16)
    width = part.shape[1]
    put(slice(0, width), code)
    side = jnp.broadcast_to(power, (part.shape[0], SIDE))
    put(slice(width, width + SIDE), side.astype(i32).astype(i16))


def decode(code):
    width = code.shape[-1] - SIDE
    return code[..., :width].astype(f32) * jnp.exp2(code[..., width : width + 1].astype(f32))


def code_rows(source, target):
    def body(r, _):
        span = pl.ds(pl.multiple_of(r * GROUP, GROUP), GROUP)

        def put(cols, value):
            target[span, cols] = value

        store_code(source(span), put)
        return 0

    lax.fori_loop(0, target.shape[0] // GROUP, body, 0)


def logits_kernel(nx, tile, pos, near, far, table, table_far, *refs):
    codes, (own, part) = refs[:-2], refs[-2:]
    step = pl.program_id(0)
    rows, width = near.shape[3:]
    columns = pl.ds(pl.multiple_of(step * tile, tile), tile)
    left = near[...].reshape(nx * rows, width)
    right = far[...].reshape(nx * rows, width)
    out = matmul(left, table[...], 1, 1) + matmul(right, table_far[...], 1, 1)
    part[:, :, columns] = out.reshape(nx, rows, tile)

    @pl.when(step == pl.num_programs(0) - 1)
    def _():
        x = pos[0]
        for k, code in enumerate(codes, 1):
            to = lax.rem(x + k, nx)
            code_rows(lambda span, to=to: part[to, span, :], code)
        own[...] = part[x]


def partial_logits(pos, near, far, table, table_far, chunk):
    _, nx, nc, rows, width = near.shape
    owner_rows = table.shape[0]
    tile = owner_rows // TILES
    return pl.pallas_call(
        functools.partial(logits_kernel, nx, tile),
        grid_spec=pltpu.PrefetchScalarGridSpec(
            num_scalar_prefetch=1,
            grid=(owner_rows // tile,),
            in_specs=[
                pl.BlockSpec((1, nx, 1, rows, width), lambda t, pos: (chunk, 0, pos[1], 0, 0)),
                pl.BlockSpec((1, nx, rows, width), lambda t, pos: (chunk, 0, 0, 0)),
                pl.BlockSpec((tile, width), lambda t, pos: (t, 0)),
                pl.BlockSpec((tile, width), lambda t, pos: (t, 0)),
            ],
            out_specs=[pl.BlockSpec((rows, owner_rows + SIDE), lambda t, pos: (0, 0))] * (nx - 1)
            + [pl.BlockSpec((rows, owner_rows), lambda t, pos: (0, 0))],
            scratch_shapes=[pltpu.VMEM((nx, rows, owner_rows), f32)],
        ),
        out_shape=[jax.ShapeDtypeStruct((rows, owner_rows + SIDE), i16)] * (nx - 1)
        + [jax.ShapeDtypeStruct((rows, owner_rows), f32)],
        compiler_params=pltpu.CompilerParams(vmem_limit_bytes=VMEM),
        cost_estimate=pl.CostEstimate(
            flops=12 * nx * rows * width * owner_rows, bytes_accessed=16 << 20, transcendentals=0
        ),
    )(pos, near, far, table, table_far)


def hidden_kernel(nx, tile, pos, grads, table, *refs):
    codes, (own, part) = refs[:-2], refs[-2:]
    step = pl.program_id(0)
    columns = pl.ds(pl.multiple_of(step * tile, tile), tile)
    out = matmul(grads[...], table[...], 1, 0)
    part[:, :, columns] = out.reshape(nx, -1, tile)

    @pl.when(step == pl.num_programs(0) - 1)
    def _():
        y = pos[2]
        for k, code in enumerate(codes, 1):
            to = lax.rem(y + k, nx)
            code_rows(lambda span, to=to: part[to, span, :], code)
        own[...] = part[y]


def hidden_parts(pos, grads, table, nx):
    positions, owner_rows = grads.shape
    width = table.shape[1]
    tile = width // HTILES
    rows = positions // nx
    return pl.pallas_call(
        functools.partial(hidden_kernel, nx, tile),
        grid_spec=pltpu.PrefetchScalarGridSpec(
            num_scalar_prefetch=1,
            grid=(width // tile,),
            in_specs=[
                pl.BlockSpec((positions, owner_rows), lambda t, pos: (0, 0)),
                pl.BlockSpec((owner_rows, tile), lambda t, pos: (0, t)),
            ],
            out_specs=[pl.BlockSpec((rows, width + SIDE), lambda t, pos: (0, 0))] * (nx - 1)
            + [pl.BlockSpec((rows, width), lambda t, pos: (0, 0))],
            scratch_shapes=[pltpu.VMEM((nx, rows, width), f32)],
        ),
        out_shape=[jax.ShapeDtypeStruct((rows, width + SIDE), i16)] * (nx - 1)
        + [jax.ShapeDtypeStruct((rows, width), f32)],
        compiler_params=pltpu.CompilerParams(vmem_limit_bytes=VMEM),
        cost_estimate=pl.CostEstimate(
            flops=6 * positions * width * owner_rows, bytes_accessed=8 << 20, transcendentals=0
        ),
    )(pos, grads, table)


def add_kernel(own, a, b, c, *rest):
    code = rest[-1]
    part = own[...]
    for ref in (a, b, c):
        part = part + decode(ref[...])

    def put(cols, value):
        code[:, :, cols] = value.reshape(code.shape[0], code.shape[1], -1)

    store_code(part, put)


def add_and_code(own, arrived, pieces, after=()):
    rows, width = own.shape
    whole = pl.BlockSpec(memory_space=pltpu.VMEM)
    return pl.pallas_call(
        add_kernel,
        in_specs=[whole] * 4 + [pl.BlockSpec(memory_space=pl.ANY)] * len(after),
        out_specs=whole,
        out_shape=jax.ShapeDtypeStruct((pieces, rows // pieces, width + SIDE), i16),
        compiler_params=pltpu.CompilerParams(vmem_limit_bytes=VMEM),
    )(own, *arrived, *after)


def sum_kernel(own, a, b, c, out):
    total = own[...]
    for ref in (a, b, c):
        total = total + decode(ref[...])
    out[...] = total


def sum_codes(own, arrived):
    return pl.pallas_call(
        sum_kernel,
        out_shape=jax.ShapeDtypeStruct(own.shape, f32),
        compiler_params=pltpu.CompilerParams(vmem_limit_bytes=VMEM),
        cost_estimate=pl.CostEstimate(flops=12 << 30, bytes_accessed=4 << 20, transcendentals=0),
    )(own, *arrived)


def slots_of(subset_ids, owner_rows, vocab_count, capacity):
    count = subset_ids.shape[0]
    owner_of = subset_ids // owner_rows
    onehot = (owner_of[:, None] == jnp.arange(vocab_count)[None, :]).astype(bf16)
    earlier = (jnp.arange(count)[:, None] > jnp.arange(count)[None, :]).astype(bf16)
    before = matmul(earlier, onehot, 1, 0)
    rank = jnp.sum(before * onehot.astype(f32), axis=1).astype(i32)
    return owner_of * capacity + rank, subset_ids % owner_rows


def on_device(hidden, table, subset_ids, targets):
    nx, nc, ny, nz = (lax.axis_size(a) for a in ("x", "core", "y", "z"))
    x, core, y = (lax.axis_index(a) for a in ("x", "core", "y"))
    pos = jnp.stack([x, core, y]).astype(i32)
    vocab_count = ny * nz
    positions, width = hidden.shape
    owner_rows = table.shape[0]
    sub_dev = subset_ids.shape[0]
    pos_dev = targets.shape[0]
    capacity = 2 * sub_dev // vocab_count
    slots = vocab_count * capacity
    out_pos = positions // vocab_count
    small = out_pos // CHUNKS
    rows = pos_dev // CHUNKS

    table_far = lax.ppermute(table, "core", SWAP)
    ordered = hidden.reshape(nx, nc, pos_dev // out_pos, CHUNKS, small, width)
    ordered = ordered.transpose(3, 0, 1, 2, 4, 5).reshape(CHUNKS, nx, nc, rows, width)
    far = lax.dynamic_index_in_dim(ordered, 1 - core, 2, keepdims=False)
    far = lax.ppermute(far, "core", SWAP)

    targets = targets.reshape(pos_dev // out_pos, CHUNKS, small, sub_dev)
    targets = targets.transpose(1, 0, 2, 3).reshape(pos_dev, sub_dev)
    slot_index, local_row = slots_of(subset_ids, owner_rows, vocab_count, capacity)
    to_slot = (jnp.arange(slots)[:, None] == slot_index[None, :]).astype(bf16)
    line = lax.broadcasted_iota(i32, (-pos_dev % 128 or 128, 1), 0)
    side = jnp.where(line == 0, local_row // LOW, jnp.where(line == 1, local_row % LOW, line == 2))
    sent = jnp.concatenate([targets, side.astype(bf16)], axis=0)
    payload = matmul(to_slot, sent, 1, 1, bf16)

    parts = []
    for c in range(CHUNKS):
        if c:
            far, codes[0] = lax.optimization_barrier((far, codes[0]))
        *codes, own = partial_logits(pos, ordered, far, table, table_far, c)
        parts.append(
            [own] + [lax.ppermute(codes[k - 1], "x", shift("x", k)) for k in (2, 1, 3)]
        )

    payload, parts[0][0] = lax.optimization_barrier((payload, parts[0][0]))
    got = lax.all_to_all(
        payload.reshape(vocab_count, capacity, -1), VOCAB, split_axis=0, concat_axis=0, tiled=True
    ).reshape(slots, -1)
    logits = [sum_codes(parts[0][0], parts[0][1:])]
    got, logits[0] = lax.optimization_barrier((got, logits[0]))
    info = got[:, pos_dev : pos_dev + 3].astype(i32)
    row_of = jnp.where(info[:, 2] > 0, info[:, 0] * LOW + info[:, 1], -1)
    to_row = (row_of[:, None] == jnp.arange(owner_rows)[None, :]).astype(bf16)
    landed = matmul(got, to_row, 0, 0)
    chosen = landed[pos_dev + 2 : pos_dev + 3] > 0.5

    local = []
    for c in range(CHUNKS):
        if c:
            *parts[c], local[-1] = lax.optimization_barrier((*parts[c], local[-1]))
            logits.append(sum_codes(parts[c][0], parts[c][1:]))
        here = logits[c]
        peak = jnp.max(jnp.where(chosen, here, FAR), axis=1)
        total = jnp.sum(jnp.where(chosen, jnp.exp(here - peak[:, None]), 0.0), axis=1)
        local.append(jnp.stack([peak, total, jnp.sum(landed[c * rows : (c + 1) * rows], axis=1)]))
    stats = jnp.stack(local).reshape(1, CHUNKS * 3 * rows)
    stats = jnp.broadcast_to(stats, (vocab_count,) + stats.shape[1:])
    stats = lax.all_to_all(stats, VOCAB, split_axis=0, concat_axis=0, tiled=True)
    stats = stats.reshape(vocab_count, CHUNKS, 3, rows)
    row_peak = jnp.max(stats[:, :, 0], axis=0)
    row_total = jnp.sum(stats[:, :, 1] * jnp.exp(stats[:, :, 0] - row_peak[None]), axis=0)
    row_mass = jnp.sum(stats[:, :, 2], axis=0)
    mine = []
    for c in range(CHUNKS):
        if c:
            row_peak, *_ = lax.optimization_barrier((row_peak, *mine))
        probs = jnp.exp(logits[c] - row_peak[c][:, None]) / row_total[c][:, None]
        grad = LOSS_SCALE * (probs * row_mass[c][:, None] - landed[c * rows : (c + 1) * rows])
        mine.append(jnp.where(chosen, grad, 0.0).astype(bf16))

    gathered = [
        lax.all_gather(g, ROWS, axis=0, tiled=True) for g in mine
    ]
    out = matmul(to_row, jnp.concatenate(logits, axis=0).astype(bf16), 1, 1, bf16)
    out = lax.all_to_all(
        out.reshape(vocab_count, capacity, pos_dev), VOCAB, split_axis=0, concat_axis=0, tiled=True
    ).reshape(slots, pos_dev)
    out, gathered[0] = lax.optimization_barrier((out, gathered[0]))

    pieces = []
    table_grad = 0.0
    for c in range(CHUNKS):
        *codes, own = hidden_parts(pos, gathered[c], table, nx)
        arrived = [lax.ppermute(codes[k - 1], "y", shift("y", k)) for k in (2, 1, 3)]
        table_grad = table_grad + matmul(
            gathered[c], ordered[c].reshape(positions // CHUNKS, width), 0, 0
        )
        after = ()
        if c == CHUNKS - 1:
            table_grad = table_grad.astype(bf16)
            after = (table_grad,)
        code = add_and_code(own, arrived, nz, after)
        code = lax.all_to_all(code, "z", split_axis=0, concat_axis=0, tiled=True)
        pieces.append(jnp.sum(decode(code), axis=0).astype(bf16))
    hidden_grad = jnp.concatenate(pieces, axis=0)

    draft = matmul(out, to_slot, 0, 0, bf16)
    draft = draft.reshape(CHUNKS, pos_dev // out_pos, small, sub_dev).transpose(1, 0, 2, 3)
    return draft.reshape(pos_dev, sub_dev), hidden_grad, table_grad


def solution(mesh):
    fine = Mesh(mesh.devices.reshape(4, 2, 4, 8), ROWS + VOCAB)
    return jax.shard_map(
        on_device,
        mesh=fine,
        in_specs=(P(None, ROWS), P(VOCAB, ROWS), P(VOCAB), P(ROWS, VOCAB)),
        out_specs=(P(ROWS, VOCAB), P(VOCAB, ROWS), P(VOCAB, ROWS)),
        check_vma=False,
    )
```

```python
import functools

import jax
import jax.numpy as jnp
from jax import lax
from jax.experimental import pallas as pl
from jax.experimental.pallas import tpu as pltpu
from jax.sharding import Mesh, PartitionSpec as P

LOSS_SCALE = 32.0
LOW = 64
GROUP = 96
TILES = 4
HTILES = 4
FAR = -3.0e38
SIDE = 128
CHUNKS = 2
ROWS = ("x", "core")
VOCAB = ("y", "z")
VMEM = 24 * 1024 * 1024
f32, bf16, i32, i16 = jnp.float32, jnp.bfloat16, jnp.int32, jnp.int16
SWAP = [(0, 1), (1, 0)]


def shift(axis, by):
    n = lax.axis_size(axis)
    return [(i, (i + by) % n) for i in range(n)]


def matmul(a, b, ca, cb, dtype=f32):
    return lax.dot_general(a, b, (((ca,), (cb,)), ((), ())), preferred_element_type=dtype)


def store_code(part, put):
    top = jnp.maximum(jnp.max(jnp.abs(part), axis=1, keepdims=True), 1e-30) * 1.0001
    power = jnp.ceil(jnp.log(top) * 1.4426950408889634) - 15.0
    code = jnp.round(part * jnp.exp2(-power)).astype(i32).astype(i16)
    width = part.shape[1]
    put(slice(0, width), code)
    side = jnp.broadcast_to(power, (part.shape[0], SIDE))
    put(slice(width, width + SIDE), side.astype(i32).astype(i16))


def decode(code):
    width = code.shape[-1] - SIDE
    return code[..., :width].astype(f32) * jnp.exp2(code[..., width : width + 1].astype(f32))


def code_rows(source, target):
    def body(r, _):
        span = pl.ds(pl.multiple_of(r * GROUP, GROUP), GROUP)

        def put(cols, value):
            target[span, cols] = value

        store_code(source(span), put)
        return 0

    lax.fori_loop(0, target.shape[0] // GROUP, body, 0)


def logits_kernel(nx, tile, pos, near, far, table, table_far, *refs):
    codes, (own, part) = refs[:-2], refs[-2:]
    step = pl.program_id(0)
    rows, width = near.shape[3:]
    columns = pl.ds(pl.multiple_of(step * tile, tile), tile)
    left = near[...].reshape(nx * rows, width)
    right = far[...].reshape(nx * rows, width)
    out = matmul(left, table[...], 1, 1) + matmul(right, table_far[...], 1, 1)
    part[:, :, columns] = out.reshape(nx, rows, tile)

    @pl.when(step == pl.num_programs(0) - 1)
    def _():
        x = pos[0]
        for k, code in enumerate(codes, 1):
            to = lax.rem(x + k, nx)
            code_rows(lambda span, to=to: part[to, span, :], code)
        own[...] = part[x]


def partial_logits(pos, near, far, table, table_far, chunk):
    _, nx, nc, rows, width = near.shape
    owner_rows = table.shape[0]
    tile = owner_rows // TILES
    return pl.pallas_call(
        functools.partial(logits_kernel, nx, tile),
        grid_spec=pltpu.PrefetchScalarGridSpec(
            num_scalar_prefetch=1,
            grid=(owner_rows // tile,),
            in_specs=[
                pl.BlockSpec((1, nx, 1, rows, width), lambda t, pos: (chunk, 0, pos[1], 0, 0)),
                pl.BlockSpec((1, nx, rows, width), lambda t, pos: (chunk, 0, 0, 0)),
                pl.BlockSpec((tile, width), lambda t, pos: (t, 0)),
                pl.BlockSpec((tile, width), lambda t, pos: (t, 0)),
            ],
            out_specs=[pl.BlockSpec((rows, owner_rows + SIDE), lambda t, pos: (0, 0))] * (nx - 1)
            + [pl.BlockSpec((rows, owner_rows), lambda t, pos: (0, 0))],
            scratch_shapes=[pltpu.VMEM((nx, rows, owner_rows), f32)],
        ),
        out_shape=[jax.ShapeDtypeStruct((rows, owner_rows + SIDE), i16)] * (nx - 1)
        + [jax.ShapeDtypeStruct((rows, owner_rows), f32)],
        compiler_params=pltpu.CompilerParams(vmem_limit_bytes=VMEM),
        cost_estimate=pl.CostEstimate(
            flops=12 * nx * rows * width * owner_rows, bytes_accessed=16 << 20, transcendentals=0
        ),
    )(pos, near, far, table, table_far)


def hidden_kernel(nx, tile, pos, here, there, table, *refs):
    codes, (own, part) = refs[:-2], refs[-2:]
    step = pl.program_id(0)
    x, core, y = pos[0], pos[1], pos[2]
    rows, owner_rows = here.shape[1:]
    columns = pl.ds(pl.multiple_of(step * tile, tile), tile)
    for grads, where in ((here, core), (there, 1 - core)):
        out = matmul(grads[...].reshape(nx * rows, owner_rows), table[...], 1, 0)
        span = pl.ds(pl.multiple_of(where * rows, rows), rows)
        for j in range(nx):
            part[lax.rem(x + j, nx), span, columns] = out[j * rows : (j + 1) * rows]

    @pl.when(step == pl.num_programs(0) - 1)
    def _():
        for k, code in enumerate(codes, 1):
            to = lax.rem(y + k, nx)
            code_rows(lambda span, to=to: part[to, span, :], code)
        own[...] = part[y]


def hidden_parts(pos, here, there, table):
    nx, rows, owner_rows = here.shape
    width = table.shape[1]
    tile = width // HTILES
    block = pl.BlockSpec((nx, rows, owner_rows), lambda t, pos: (0, 0, 0))
    return pl.pallas_call(
        functools.partial(hidden_kernel, nx, tile),
        grid_spec=pltpu.PrefetchScalarGridSpec(
            num_scalar_prefetch=1,
            grid=(width // tile,),
            in_specs=[block, block, pl.BlockSpec((owner_rows, tile), lambda t, pos: (0, t))],
            out_specs=[pl.BlockSpec((2 * rows, width + SIDE), lambda t, pos: (0, 0))] * (nx - 1)
            + [pl.BlockSpec((2 * rows, width), lambda t, pos: (0, 0))],
            scratch_shapes=[pltpu.VMEM((nx, 2 * rows, width), f32)],
        ),
        out_shape=[jax.ShapeDtypeStruct((2 * rows, width + SIDE), i16)] * (nx - 1)
        + [jax.ShapeDtypeStruct((2 * rows, width), f32)],
        compiler_params=pltpu.CompilerParams(vmem_limit_bytes=VMEM),
        cost_estimate=pl.CostEstimate(
            flops=nx * rows * width, bytes_accessed=1 << 10, transcendentals=0
        ),
    )(pos, here, there, table)


def add_kernel(first, own, a, b, c, _, code):
    part = own[...]
    for ref in (a, b, c):
        part = part + decode(ref[...])
    pieces = code.shape[0]
    part = jnp.concatenate(
        [p.reshape(pieces, -1, p.shape[1]) for p in (first[...], part)], axis=1
    )

    def put(cols, value):
        code[:, :, cols] = value.reshape(code.shape[0], code.shape[1], -1)

    store_code(part.reshape(-1, part.shape[2]), put)


def add_and_code(first, own, arrived, pieces, after):
    rows, width = own.shape
    whole = pl.BlockSpec(memory_space=pltpu.VMEM)
    shape = (pieces, CHUNKS * rows // pieces, width + SIDE)
    return pl.pallas_call(
        add_kernel,
        in_specs=[whole] * 5 + [pl.BlockSpec(memory_space=pl.ANY)],
        out_specs=whole,
        out_shape=jax.ShapeDtypeStruct(shape, i16),
        compiler_params=pltpu.CompilerParams(vmem_limit_bytes=VMEM),
        cost_estimate=pl.CostEstimate(flops=4 << 30, bytes_accessed=8 << 20, transcendentals=0),
    )(first, own, *arrived, after)


def sum_kernel(own, a, b, c, out):
    total = own[...]
    for ref in (a, b, c):
        total = total + decode(ref[...])
    out[...] = total


def sum_codes(own, arrived):
    return pl.pallas_call(
        sum_kernel,
        out_shape=jax.ShapeDtypeStruct(own.shape, f32),
        compiler_params=pltpu.CompilerParams(vmem_limit_bytes=VMEM),
        cost_estimate=pl.CostEstimate(flops=12 << 30, bytes_accessed=4 << 20, transcendentals=0),
    )(own, *arrived)


def slots_of(subset_ids, owner_rows, vocab_count, capacity):
    count = subset_ids.shape[0]
    owner_of = subset_ids // owner_rows
    onehot = (owner_of[:, None] == jnp.arange(vocab_count)[None, :]).astype(bf16)
    earlier = (jnp.arange(count)[:, None] > jnp.arange(count)[None, :]).astype(bf16)
    before = matmul(earlier, onehot, 1, 0)
    rank = jnp.sum(before * onehot.astype(f32), axis=1).astype(i32)
    return owner_of * capacity + rank, subset_ids % owner_rows


def on_device(hidden, table, subset_ids, targets):
    nx, nc, ny, nz = (lax.axis_size(a) for a in ("x", "core", "y", "z"))
    x, core, y = (lax.axis_index(a) for a in ("x", "core", "y"))
    pos = jnp.stack([x, core, y]).astype(i32)
    vocab_count = ny * nz
    positions, width = hidden.shape
    owner_rows = table.shape[0]
    sub_dev = subset_ids.shape[0]
    pos_dev = targets.shape[0]
    capacity = 2 * sub_dev // vocab_count
    slots = vocab_count * capacity
    out_pos = positions // vocab_count
    small = out_pos // CHUNKS
    rows = pos_dev // CHUNKS

    table_far = lax.ppermute(table, "core", SWAP)
    ordered = hidden.reshape(nx, nc, pos_dev // out_pos, CHUNKS, small, width)
    ordered = ordered.transpose(3, 0, 1, 2, 4, 5).reshape(CHUNKS, nx, nc, rows, width)
    far = lax.dynamic_index_in_dim(ordered, 1 - core, 2, keepdims=False)
    far = lax.ppermute(far, "core", SWAP)

    targets = targets.reshape(pos_dev // out_pos, CHUNKS, small, sub_dev)
    targets = targets.transpose(1, 0, 2, 3).reshape(pos_dev, sub_dev)
    slot_index, local_row = slots_of(subset_ids, owner_rows, vocab_count, capacity)
    to_slot = (jnp.arange(slots)[:, None] == slot_index[None, :]).astype(bf16)
    line = lax.broadcasted_iota(i32, (-pos_dev % 128 or 128, 1), 0)
    side = jnp.where(line == 0, local_row // LOW, jnp.where(line == 1, local_row % LOW, line == 2))
    sent = jnp.concatenate([targets, side.astype(bf16)], axis=0)
    payload = matmul(to_slot, sent, 1, 1, bf16)
    payload, far = lax.optimization_barrier((payload, far))
    got = lax.all_to_all(
        payload.reshape(vocab_count, capacity, -1), VOCAB, split_axis=0, concat_axis=0, tiled=True
    ).reshape(slots, -1)

    parts = []
    for c in range(CHUNKS):
        if c:
            far, parts[0][0] = lax.optimization_barrier((far, parts[0][0]))
        *codes, own = partial_logits(pos, ordered, far, table, table_far, c)
        parts.append(
            [own] + [lax.ppermute(codes[k - 1], "x", shift("x", k)) for k in (2, 1, 3)]
        )

    logits = [sum_codes(parts[0][0], parts[0][1:])]
    got, later, logits[0] = lax.optimization_barrier((got, ordered, logits[0]))
    info = got[:, pos_dev : pos_dev + 3].astype(i32)
    row_of = jnp.where(info[:, 2] > 0, info[:, 0] * LOW + info[:, 1], -1)
    to_row = (row_of[:, None] == jnp.arange(owner_rows)[None, :]).astype(bf16)
    landed = matmul(got, to_row, 0, 0)
    chosen = landed[pos_dev + 2 : pos_dev + 3] > 0.5

    local = []
    for c in range(CHUNKS):
        if c:
            *parts[c], local[-1] = lax.optimization_barrier((*parts[c], local[-1]))
            logits.append(sum_codes(parts[c][0], parts[c][1:]))
        here = logits[c]
        peak = jnp.max(jnp.where(chosen, here, FAR), axis=1)
        total = jnp.sum(jnp.where(chosen, jnp.exp(here - peak[:, None]), 0.0), axis=1)
        local.append(jnp.stack([peak, total, jnp.sum(landed[c * rows : (c + 1) * rows], axis=1)]))
    stats = jnp.stack(local).reshape(1, CHUNKS * 3 * rows)
    stats = jnp.broadcast_to(stats, (vocab_count,) + stats.shape[1:])
    stats = lax.all_to_all(stats, VOCAB, split_axis=0, concat_axis=0, tiled=True)
    stats = stats.reshape(vocab_count, CHUNKS, 3, rows)
    row_peak = jnp.max(stats[:, :, 0], axis=0)
    row_total = jnp.sum(stats[:, :, 1] * jnp.exp(stats[:, :, 0] - row_peak[None]), axis=0)
    row_mass = jnp.sum(stats[:, :, 2], axis=0)
    mine = []
    for c in range(CHUNKS):
        if c:
            row_peak, *_ = lax.optimization_barrier((row_peak, *mine))
        probs = jnp.exp(logits[c] - row_peak[c][:, None]) / row_total[c][:, None]
        grad = LOSS_SCALE * (probs * row_mass[c][:, None] - landed[c * rows : (c + 1) * rows])
        mine.append(jnp.where(chosen, grad, 0.0).astype(bf16))

    out = matmul(to_row, jnp.concatenate(logits, axis=0).astype(bf16), 1, 1, bf16)

    blocks = []
    terms = []
    sums = []
    for c in range(CHUNKS):
        blocks = [lax.ppermute(mine[c], "x", shift("x", -j)) for j in range(1, nx)]
        if c == 0:
            out, mine[1], *blocks = lax.optimization_barrier((out, mine[1], *blocks))
        else:
            sums[0], *blocks = lax.optimization_barrier((sums[0], *blocks))
        here = jnp.stack([mine[c]] + blocks)
        there = lax.ppermute(here, "core", SWAP)
        *codes, own = hidden_parts(pos, here, there, table)
        sums += ([own] + [lax.ppermute(codes[k - 1], "y", shift("y", k)) for k in (2, 1, 3)])
        if c == 0:
            out, sums[0] = lax.optimization_barrier((out, sums[0]))
            back = lax.all_to_all(
                out.reshape(vocab_count, capacity, pos_dev),
                VOCAB,
                split_axis=0,
                concat_axis=0,
                tiled=True,
            ).reshape(slots, pos_dev)
        terms += [here, there]
    sums[:5] = lax.optimization_barrier(tuple(sums[:5]))
    first = sum_codes(sums[0], sums[1:4])
    first, terms[0] = lax.optimization_barrier((first, terms[0]))
    turned = jnp.stack(
        [lax.dynamic_index_in_dim(later, (x + j) % nx, 1, False) for j in range(nx)], 1
    )
    turned = [lax.dynamic_index_in_dim(turned, i, 2, False) for i in (core, 1 - core)]
    table_grad = matmul(
        jnp.concatenate(terms).reshape(positions, owner_rows),
        jnp.stack(turned, 1).reshape(positions, width),
        0,
        0,
        bf16,
    )
    code = add_and_code(first, sums[4], sums[5:], nz, table_grad)
    code = lax.all_to_all(code, "z", split_axis=0, concat_axis=0, tiled=True)
    hidden_grad = jnp.sum(decode(code), axis=0).astype(bf16)

    draft = matmul(back, to_slot, 0, 0, bf16)
    draft = draft.reshape(CHUNKS, pos_dev // out_pos, small, sub_dev).transpose(1, 0, 2, 3)
    return draft.reshape(pos_dev, sub_dev), hidden_grad, table_grad


def solution(mesh):
    fine = Mesh(mesh.devices.reshape(4, 2, 4, 8), ROWS + VOCAB)
    return jax.shard_map(
        on_device,
        mesh=fine,
        in_specs=(P(None, ROWS), P(VOCAB, ROWS), P(VOCAB), P(ROWS, VOCAB)),
        out_specs=(P(ROWS, VOCAB), P(VOCAB, ROWS), P(VOCAB, ROWS)),
        check_vma=False,
    )
```

```python
import functools

import jax
import jax.numpy as jnp
from jax import lax
from jax.experimental import pallas as pl
from jax.experimental.pallas import tpu as pltpu
from jax.sharding import Mesh, PartitionSpec as P

LOSS_SCALE = 32.0
LOW = 64
GROUP = 96
TILES = 4
HTILES = 4
FAR = -3.0e38
SIDE = 128
CHUNKS = 2
ROWS = ("x", "core")
VOCAB = ("y", "z")
VMEM = 24 * 1024 * 1024
LARGE = 56 * 1024 * 1024
f32, bf16, i32, i16 = jnp.float32, jnp.bfloat16, jnp.int32, jnp.int16
SWAP = [(0, 1), (1, 0)]


def shift(axis, by):
    n = lax.axis_size(axis)
    return [(i, (i + by) % n) for i in range(n)]


def matmul(a, b, ca, cb, dtype=f32):
    return lax.dot_general(a, b, (((ca,), (cb,)), ((), ())), preferred_element_type=dtype)


def store_code(part, put):
    top = jnp.maximum(jnp.max(jnp.abs(part), axis=1, keepdims=True), 1e-30) * 1.0001
    power = jnp.ceil(jnp.log(top) * 1.4426950408889634) - 15.0
    code = jnp.round(part * jnp.exp2(-power)).astype(i32).astype(i16)
    width = part.shape[1]
    put(slice(0, width), code)
    side = jnp.broadcast_to(power, (part.shape[0], SIDE))
    put(slice(width, width + SIDE), side.astype(i32).astype(i16))


def decode(code):
    width = code.shape[-1] - SIDE
    return code[..., :width].astype(f32) * jnp.exp2(code[..., width : width + 1].astype(f32))


def code_rows(source, target):
    def body(r, _):
        span = pl.ds(pl.multiple_of(r * GROUP, GROUP), GROUP)

        def put(cols, value):
            target[span, cols] = value

        store_code(source(span), put)
        return 0

    lax.fori_loop(0, target.shape[0] // GROUP, body, 0)


def logits_kernel(nx, tile, pos, near, far, table, table_far, *refs):
    codes, (own, part) = refs[:-2], refs[-2:]
    step = pl.program_id(0)
    rows, width = near.shape[3:]
    columns = pl.ds(pl.multiple_of(step * tile, tile), tile)
    left = near[...].reshape(nx * rows, width)
    right = far[...].reshape(nx * rows, width)
    out = matmul(left, table[...], 1, 1) + matmul(right, table_far[...], 1, 1)
    part[:, :, columns] = out.reshape(nx, rows, tile)

    @pl.when(step == pl.num_programs(0) - 1)
    def _():
        x = pos[0]
        for k, code in enumerate(codes, 1):
            to = lax.rem(x + k, nx)
            code_rows(lambda span, to=to: part[to, span, :], code)
        own[...] = part[x]


def partial_logits(pos, near, far, table, table_far, chunk):
    _, nx, nc, rows, width = near.shape
    owner_rows = table.shape[0]
    tile = owner_rows // TILES
    return pl.pallas_call(
        functools.partial(logits_kernel, nx, tile),
        grid_spec=pltpu.PrefetchScalarGridSpec(
            num_scalar_prefetch=1,
            grid=(owner_rows // tile,),
            in_specs=[
                pl.BlockSpec((1, nx, 1, rows, width), lambda t, pos: (chunk, 0, pos[1], 0, 0)),
                pl.BlockSpec((1, nx, rows, width), lambda t, pos: (chunk, 0, 0, 0)),
                pl.BlockSpec((tile, width), lambda t, pos: (t, 0)),
                pl.BlockSpec((tile, width), lambda t, pos: (t, 0)),
            ],
            out_specs=[pl.BlockSpec((rows, owner_rows + SIDE), lambda t, pos: (0, 0))] * (nx - 1)
            + [pl.BlockSpec((rows, owner_rows), lambda t, pos: (0, 0))],
            scratch_shapes=[pltpu.VMEM((nx, rows, owner_rows), f32)],
        ),
        out_shape=[jax.ShapeDtypeStruct((rows, owner_rows + SIDE), i16)] * (nx - 1)
        + [jax.ShapeDtypeStruct((rows, owner_rows), f32)],
        compiler_params=pltpu.CompilerParams(vmem_limit_bytes=LARGE),
        cost_estimate=pl.CostEstimate(
            flops=12 * nx * rows * width * owner_rows, bytes_accessed=16 << 20, transcendentals=0
        ),
    )(pos, near, far, table, table_far)


def hidden_kernel(nx, tile, turned, pos, *refs):
    grads, table, codes, (own, part) = refs[: -nx - 2], refs[-nx - 2], refs[-nx - 1 : -2], refs[-2:]
    step = pl.program_id(0)
    x, core, y = pos[0], pos[1], pos[2]
    columns = pl.ds(pl.multiple_of(step * tile, tile), tile)
    for ref, where in zip(grads, (core, 1 - core)):
        rows = ref.shape[1]
        out = matmul(ref[...].reshape(nx * rows, -1), table[...], 1, 0)
        if not turned:
            part[:, :, columns] = out.reshape(nx, rows, tile)
            continue
        span = pl.ds(pl.multiple_of(where * rows, rows), rows)
        for j in range(nx):
            part[lax.rem(x + j, nx), span, columns] = out[j * rows : (j + 1) * rows]

    @pl.when(step == pl.num_programs(0) - 1)
    def _():
        for k, code in enumerate(codes, 1):
            to = lax.rem(y + k, nx)
            code_rows(lambda span, to=to: part[to, span, :], code)
        own[...] = part[y]


def hidden_parts(pos, grads, table, turned):
    nx, rows, owner_rows = grads[0].shape
    total = len(grads) * rows
    width = table.shape[1]
    tile = width // HTILES
    block = pl.BlockSpec((nx, rows, owner_rows), lambda t, pos: (0, 0, 0))
    return pl.pallas_call(
        functools.partial(hidden_kernel, nx, tile, turned),
        grid_spec=pltpu.PrefetchScalarGridSpec(
            num_scalar_prefetch=1,
            grid=(width // tile,),
            in_specs=[block] * len(grads)
            + [pl.BlockSpec((owner_rows, tile), lambda t, pos: (0, t))],
            out_specs=[pl.BlockSpec((total, width + SIDE), lambda t, pos: (0, 0))] * (nx - 1)
            + [pl.BlockSpec((total, width), lambda t, pos: (0, 0))],
            scratch_shapes=[pltpu.VMEM((nx, total, width), f32)],
        ),
        out_shape=[jax.ShapeDtypeStruct((total, width + SIDE), i16)] * (nx - 1)
        + [jax.ShapeDtypeStruct((total, width), f32)],
        compiler_params=pltpu.CompilerParams(vmem_limit_bytes=VMEM),
        cost_estimate=pl.CostEstimate(
            flops=nx * rows * width, bytes_accessed=1 << 10, transcendentals=0
        ),
    )(pos, *grads, table)


def add_kernel(own, a, b, c, *rest):
    code = rest[-1]
    part = own[...]
    for ref in (a, b, c):
        part = part + decode(ref[...])

    def put(cols, value):
        code[:, :, cols] = value.reshape(code.shape[0], code.shape[1], -1)

    store_code(part, put)


def add_and_code(own, arrived, pieces, after=()):
    rows, width = own.shape
    whole = pl.BlockSpec(memory_space=pltpu.VMEM)
    return pl.pallas_call(
        add_kernel,
        in_specs=[whole] * 4 + [pl.BlockSpec(memory_space=pl.ANY)] * len(after),
        out_specs=whole,
        out_shape=jax.ShapeDtypeStruct((pieces, rows // pieces, width + SIDE), i16),
        compiler_params=pltpu.CompilerParams(vmem_limit_bytes=LARGE),
        cost_estimate=pl.CostEstimate(flops=12 << 30, bytes_accessed=8 << 20, transcendentals=0),
    )(own, *arrived, *after)


def sum_kernel(own, a, b, c, out):
    total = own[...]
    for ref in (a, b, c):
        total = total + decode(ref[...])
    out[...] = total


def sum_codes(own, arrived):
    return pl.pallas_call(
        sum_kernel,
        out_shape=jax.ShapeDtypeStruct(own.shape, f32),
        compiler_params=pltpu.CompilerParams(vmem_limit_bytes=LARGE),
        cost_estimate=pl.CostEstimate(flops=12 << 30, bytes_accessed=4 << 20, transcendentals=0),
    )(own, *arrived)


def slots_of(subset_ids, owner_rows, vocab_count, capacity):
    count = subset_ids.shape[0]
    owner_of = subset_ids // owner_rows
    onehot = (owner_of[:, None] == jnp.arange(vocab_count)[None, :]).astype(bf16)
    earlier = (jnp.arange(count)[:, None] > jnp.arange(count)[None, :]).astype(bf16)
    before = matmul(earlier, onehot, 1, 0)
    rank = jnp.sum(before * onehot.astype(f32), axis=1).astype(i32)
    return owner_of * capacity + rank, subset_ids % owner_rows


def on_device(hidden, table, subset_ids, targets):
    nx, nc, ny, nz = (lax.axis_size(a) for a in ("x", "core", "y", "z"))
    x, core, y = (lax.axis_index(a) for a in ("x", "core", "y"))
    pos = jnp.stack([x, core, y]).astype(i32)
    vocab_count = ny * nz
    positions, width = hidden.shape
    owner_rows = table.shape[0]
    sub_dev = subset_ids.shape[0]
    pos_dev = targets.shape[0]
    capacity = 2 * sub_dev // vocab_count
    slots = vocab_count * capacity
    out_pos = positions // vocab_count
    small = out_pos // CHUNKS
    rows = pos_dev // CHUNKS

    table_far = lax.ppermute(table, "core", SWAP)
    ordered = hidden.reshape(nx, nc, pos_dev // out_pos, CHUNKS, small, width)
    ordered = ordered.transpose(3, 0, 1, 2, 4, 5).reshape(CHUNKS, nx, nc, rows, width)
    far = lax.dynamic_index_in_dim(ordered, 1 - core, 2, keepdims=False)
    far = lax.ppermute(far, "core", SWAP)

    targets = targets.reshape(pos_dev // out_pos, CHUNKS, small, sub_dev)
    targets = targets.transpose(1, 0, 2, 3).reshape(pos_dev, sub_dev)
    slot_index, local_row = slots_of(subset_ids, owner_rows, vocab_count, capacity)
    to_slot = (jnp.arange(slots)[:, None] == slot_index[None, :]).astype(bf16)
    line = lax.broadcasted_iota(i32, (-pos_dev % 128 or 128, 1), 0)
    side = jnp.where(line == 0, local_row // LOW, jnp.where(line == 1, local_row % LOW, line == 2))
    sent = jnp.concatenate([targets, side.astype(bf16)], axis=0)
    payload = matmul(to_slot, sent, 1, 1, bf16)
    payload, far = lax.optimization_barrier((payload, far))
    got = lax.all_to_all(
        payload.reshape(vocab_count, capacity, -1), VOCAB, split_axis=0, concat_axis=0, tiled=True
    ).reshape(slots, -1)

    parts = []
    for c in range(CHUNKS):
        if c:
            far, parts[0][0] = lax.optimization_barrier((far, parts[0][0]))
        *codes, own = partial_logits(pos, ordered, far, table, table_far, c)
        parts.append(
            [own] + [lax.ppermute(codes[k - 1], "x", shift("x", k)) for k in (2, 1, 3)]
        )

    logits = [sum_codes(parts[0][0], parts[0][1:])]
    got, later, logits[0] = lax.optimization_barrier((got, ordered, logits[0]))
    info = got[:, pos_dev : pos_dev + 3].astype(i32)
    row_of = jnp.where(info[:, 2] > 0, info[:, 0] * LOW + info[:, 1], -1)
    to_row = (row_of[:, None] == jnp.arange(owner_rows)[None, :]).astype(bf16)
    landed = matmul(got, to_row, 0, 0)
    chosen = landed[pos_dev + 2 : pos_dev + 3] > 0.5

    order = [lax.dynamic_index_in_dim(later[0], (x + j) % nx, 0, False) for j in range(nx)]
    order = jnp.stack(order)
    order = [lax.dynamic_index_in_dim(order, i, 1, False) for i in (core, 1 - core)]
    order = jnp.concatenate(order).reshape(-1, width)
    order, *parts[1] = lax.optimization_barrier((order, *parts[1]))
    local = []
    for c in range(CHUNKS):
        if c:
            *parts[c], local[-1] = lax.optimization_barrier((*parts[c], local[-1]))
            logits.append(sum_codes(parts[c][0], parts[c][1:]))
        here = logits[c]
        peak = jnp.max(jnp.where(chosen, here, FAR), axis=1)
        total = jnp.sum(jnp.where(chosen, jnp.exp(here - peak[:, None]), 0.0), axis=1)
        local.append(jnp.stack([peak, total, jnp.sum(landed[c * rows : (c + 1) * rows], axis=1)]))
    stats = jnp.stack(local).reshape(1, CHUNKS * 3 * rows)
    stats = jnp.broadcast_to(stats, (vocab_count,) + stats.shape[1:])
    stats = lax.all_to_all(stats, VOCAB, split_axis=0, concat_axis=0, tiled=True)
    stats = stats.reshape(vocab_count, CHUNKS, 3, rows)
    row_peak = jnp.max(stats[:, :, 0], axis=0)
    row_total = jnp.sum(stats[:, :, 1] * jnp.exp(stats[:, :, 0] - row_peak[None]), axis=0)
    row_mass = jnp.sum(stats[:, :, 2], axis=0)
    mine = []
    for c in range(CHUNKS):
        if c:
            row_peak, *_ = lax.optimization_barrier((row_peak, *mine))
        probs = jnp.exp(logits[c] - row_peak[c][:, None]) / row_total[c][:, None]
        grad = LOSS_SCALE * (probs * row_mass[c][:, None] - landed[c * rows : (c + 1) * rows])
        mine.append(jnp.where(chosen, grad, 0.0).astype(bf16))

    out = matmul(to_row, jnp.concatenate(logits, axis=0).astype(bf16), 1, 1, bf16)

    blocks = [lax.ppermute(mine[0], "x", shift("x", -j)) for j in range(1, nx)]
    whole = lax.all_gather(mine[1], ROWS, axis=0, tiled=True).reshape(nx, nc * rows, owner_rows)
    out, *blocks = lax.optimization_barrier((out, *blocks))
    back = lax.all_to_all(
        out.reshape(vocab_count, capacity, pos_dev), VOCAB, split_axis=0, concat_axis=0, tiled=True
    ).reshape(slots, pos_dev)
    here = jnp.stack([mine[0]] + blocks)
    there = lax.ppermute(here, "core", SWAP)

    pieces = []
    for c, grads in enumerate(((here, there), (whole,))):
        if c:
            (*sent, own), *grads = lax.optimization_barrier(((*sent, own), *grads))
        *sent, own_next = hidden_parts(pos, grads, table, c == 0)
        arrived = [lax.ppermute(sent[k - 1], "y", shift("y", k)) for k in (2, 1, 3)]
        own = own_next
        pieces.append([own, arrived])
    (pieces[0][0], pieces[1][0]) = lax.optimization_barrier((pieces[0][0], pieces[1][0]))
    terms = jnp.concatenate(
        [here.reshape(-1, owner_rows), there.reshape(-1, owner_rows), whole.reshape(-1, owner_rows)]
    )
    order = jnp.concatenate([order, later[1].reshape(-1, width)])
    table_grad = matmul(terms, order, 0, 0, bf16)
    pieces = [
        add_and_code(own, arrived, nz, (table_grad,) if c else ())
        for c, (own, arrived) in enumerate(pieces)
    ]
    pieces = [lax.all_to_all(p, "z", split_axis=0, concat_axis=0, tiled=True) for p in pieces]
    pieces = [jnp.sum(decode(p), axis=0).astype(bf16) for p in pieces]
    hidden_grad = jnp.concatenate(pieces, axis=0)

    draft = matmul(back, to_slot, 0, 0, bf16)
    draft = draft.reshape(CHUNKS, pos_dev // out_pos, small, sub_dev).transpose(1, 0, 2, 3)
    return draft.reshape(pos_dev, sub_dev), hidden_grad, table_grad


def solution(mesh):
    fine = Mesh(mesh.devices.reshape(4, 2, 4, 8), ROWS + VOCAB)
    return jax.shard_map(
        on_device,
        mesh=fine,
        in_specs=(P(None, ROWS), P(VOCAB, ROWS), P(VOCAB), P(ROWS, VOCAB)),
        out_specs=(P(ROWS, VOCAB), P(VOCAB, ROWS), P(VOCAB, ROWS)),
        check_vma=False,
    )
```

```python
import functools

import jax
import jax.numpy as jnp
from jax import lax
from jax.experimental import pallas as pl
from jax.experimental.pallas import tpu as pltpu
from jax.sharding import Mesh, PartitionSpec as P

LOSS_SCALE = 32.0
LOW = 64
GROUP = 96
TILES = 4
HTILES = 4
FAR = -3.0e38
SIDE = 128
STACK = 10
CHUNKS = 2
ROWS = ("x", "core")
VOCAB = ("y", "z")
LARGE = 56 * 1024 * 1024
f32, bf16, i32, i16 = jnp.float32, jnp.bfloat16, jnp.int32, jnp.int16
SWAP = [(0, 1), (1, 0)]


def shift(axis, by):
    n = lax.axis_size(axis)
    return [(i, (i + by) % n) for i in range(n)]


def matmul(a, b, ca, cb, dtype=f32):
    return lax.dot_general(a, b, (((ca,), (cb,)), ((), ())), preferred_element_type=dtype)


def store_code(part, put):
    top = jnp.maximum(jnp.max(jnp.abs(part), axis=1, keepdims=True), 1e-30) * 1.0001
    power = jnp.ceil(jnp.log(top) * 1.4426950408889634) - 15.0
    code = jnp.round(part * jnp.exp2(-power)).astype(i32).astype(i16)
    width = part.shape[1]
    put(slice(0, width), code)
    side = jnp.broadcast_to(power, (part.shape[0], SIDE))
    put(slice(width, width + SIDE), side.astype(i32).astype(i16))


def decode(code):
    width = code.shape[-1] - SIDE
    return code[..., :width].astype(f32) * jnp.exp2(code[..., width : width + 1].astype(f32))


def code_rows(source, target):
    def body(r, _):
        span = pl.ds(pl.multiple_of(r * GROUP, GROUP), GROUP)

        def put(cols, value):
            target[span, cols] = value

        store_code(source(span), put)
        return 0

    lax.fori_loop(0, target.shape[0] // GROUP, body, 0)


def logits_kernel(nx, tile, pos, near, far, table, table_far, *refs):
    codes, (own, part) = refs[:-2], refs[-2:]
    step = pl.program_id(0)
    rows, width = near.shape[3:]
    columns = pl.ds(pl.multiple_of(step * tile, tile), tile)
    left = near[...].reshape(nx * rows, width)
    right = far[...].reshape(nx * rows, width)
    out = matmul(left, table[...], 1, 1) + matmul(right, table_far[...], 1, 1)
    part[:, :, columns] = out.reshape(nx, rows, tile)

    @pl.when(step == pl.num_programs(0) - 1)
    def _():
        x = pos[0]
        for k, code in enumerate(codes, 1):
            to = lax.rem(x + k, nx)
            code_rows(lambda span, to=to: part[to, span, :], code)
        own[...] = part[x]


def partial_logits(pos, near, far, table, table_far, chunk):
    _, nx, nc, rows, width = near.shape
    owner_rows = table.shape[0]
    tile = owner_rows // TILES
    return pl.pallas_call(
        functools.partial(logits_kernel, nx, tile),
        grid_spec=pltpu.PrefetchScalarGridSpec(
            num_scalar_prefetch=1,
            grid=(owner_rows // tile,),
            in_specs=[
                pl.BlockSpec((1, nx, 1, rows, width), lambda t, pos: (chunk, 0, pos[1], 0, 0)),
                pl.BlockSpec((1, nx, rows, width), lambda t, pos: (chunk, 0, 0, 0)),
                pl.BlockSpec((tile, width), lambda t, pos: (t, 0)),
                pl.BlockSpec((tile, width), lambda t, pos: (t, 0)),
            ],
            out_specs=[pl.BlockSpec((rows, owner_rows + SIDE), lambda t, pos: (0, 0))] * (nx - 1)
            + [pl.BlockSpec((rows, owner_rows), lambda t, pos: (0, 0))],
            scratch_shapes=[pltpu.VMEM((nx, rows, owner_rows), f32)],
        ),
        out_shape=[jax.ShapeDtypeStruct((rows, owner_rows + SIDE), i16)] * (nx - 1)
        + [jax.ShapeDtypeStruct((rows, owner_rows), f32)],
        compiler_params=pltpu.CompilerParams(vmem_limit_bytes=LARGE),
        cost_estimate=pl.CostEstimate(
            flops=12 * nx * rows * width * owner_rows, bytes_accessed=16 << 20, transcendentals=0
        ),
    )(pos, near, far, table, table_far)


def hidden_kernel(nx, tile, turned, pos, *refs):
    grads, table, codes, (own, part) = refs[: -nx - 2], refs[-nx - 2], refs[-nx - 1 : -2], refs[-2:]
    step = pl.program_id(0)
    x, core, y = pos[0], pos[1], pos[2]
    columns = pl.ds(pl.multiple_of(step * tile, tile), tile)
    for ref, where in zip(grads, (core, 1 - core)):
        rows = ref.shape[1]
        out = matmul(ref[...].reshape(nx * rows, -1), table[...], 1, 0)
        if not turned:
            part[:, :, columns] = out.reshape(nx, rows, tile)
            continue
        span = pl.ds(pl.multiple_of(where * rows, rows), rows)
        for j in range(nx):
            part[lax.rem(x + j, nx), span, columns] = out[j * rows : (j + 1) * rows]

    @pl.when(step == pl.num_programs(0) - 1)
    def _():
        for k, code in enumerate(codes, 1):
            to = lax.rem(y + k, nx)
            code_rows(lambda span, to=to: part[to, span, :], code)
        own[...] = part[y]


def hidden_parts(pos, grads, table, turned):
    nx, rows, owner_rows = grads[0].shape
    total = len(grads) * rows
    width = table.shape[1]
    tile = width // HTILES
    block = pl.BlockSpec((nx, rows, owner_rows), lambda t, pos: (0, 0, 0))
    return pl.pallas_call(
        functools.partial(hidden_kernel, nx, tile, turned),
        grid_spec=pltpu.PrefetchScalarGridSpec(
            num_scalar_prefetch=1,
            grid=(width // tile,),
            in_specs=[block] * len(grads)
            + [pl.BlockSpec((owner_rows, tile), lambda t, pos: (0, t))],
            out_specs=[pl.BlockSpec((total, width + SIDE), lambda t, pos: (0, 0))] * (nx - 1)
            + [pl.BlockSpec((total, width), lambda t, pos: (0, 0))],
            scratch_shapes=[pltpu.VMEM((nx, total, width), f32)],
        ),
        out_shape=[jax.ShapeDtypeStruct((total, width + SIDE), i16)] * (nx - 1)
        + [jax.ShapeDtypeStruct((total, width), f32)],
        compiler_params=pltpu.CompilerParams(vmem_limit_bytes=LARGE),
        cost_estimate=pl.CostEstimate(
            flops=10 << 30, bytes_accessed=8 << 20, transcendentals=0
        ),
    )(pos, *grads, table)


def add_kernel(own, a, b, c, *rest):
    code = rest[-1]
    part = own[...]
    for ref in (a, b, c):
        part = part + decode(ref[...])

    def put(cols, value):
        code[:, :, cols] = value.reshape(code.shape[0], code.shape[1], -1)

    store_code(part, put)


def add_and_code(own, arrived, pieces, after=()):
    rows, width = own.shape
    whole = pl.BlockSpec(memory_space=pltpu.VMEM)
    return pl.pallas_call(
        add_kernel,
        in_specs=[whole] * 4 + [pl.BlockSpec(memory_space=pl.ANY)] * len(after),
        out_specs=whole,
        out_shape=jax.ShapeDtypeStruct((pieces, rows // pieces, width + SIDE), i16),
        compiler_params=pltpu.CompilerParams(vmem_limit_bytes=LARGE),
        cost_estimate=pl.CostEstimate(flops=12 << 30, bytes_accessed=8 << 20, transcendentals=0),
    )(own, *arrived, *after)


def sum_kernel(own, a, b, c, out):
    total = own[...]
    for ref in (a, b, c):
        total = total + decode(ref[...])
    out[...] = total


def sum_codes(own, arrived):
    return pl.pallas_call(
        sum_kernel,
        out_shape=jax.ShapeDtypeStruct(own.shape, f32),
        compiler_params=pltpu.CompilerParams(vmem_limit_bytes=LARGE),
        cost_estimate=pl.CostEstimate(flops=12 << 30, bytes_accessed=4 << 20, transcendentals=0),
    )(own, *arrived)


def stack_kernel(*refs):
    count = len(refs) - CHUNKS
    for c, out in enumerate(refs[count:]):
        for j in range(count):
            out[j] = refs[j][c]


def stack_chunks(blocks):
    _, rows, width = blocks[0].shape
    return pl.pallas_call(
        stack_kernel,
        out_shape=[jax.ShapeDtypeStruct((len(blocks), rows, width), bf16)] * CHUNKS,
        compiler_params=pltpu.CompilerParams(vmem_limit_bytes=LARGE),
        cost_estimate=pl.CostEstimate(flops=STACK << 30, bytes_accessed=6 << 20, transcendentals=0),
    )(*blocks)


def slots_of(subset_ids, owner_rows, vocab_count, capacity):
    count = subset_ids.shape[0]
    owner_of = subset_ids // owner_rows
    onehot = (owner_of[:, None] == jnp.arange(vocab_count)[None, :]).astype(bf16)
    earlier = (jnp.arange(count)[:, None] > jnp.arange(count)[None, :]).astype(bf16)
    before = matmul(earlier, onehot, 1, 0)
    rank = jnp.sum(before * onehot.astype(f32), axis=1).astype(i32)
    return owner_of * capacity + rank, subset_ids % owner_rows


def on_device(hidden, table, subset_ids, targets):
    nx, nc, ny, nz = (lax.axis_size(a) for a in ("x", "core", "y", "z"))
    x, core, y = (lax.axis_index(a) for a in ("x", "core", "y"))
    pos = jnp.stack([x, core, y]).astype(i32)
    vocab_count = ny * nz
    positions, width = hidden.shape
    owner_rows = table.shape[0]
    sub_dev = subset_ids.shape[0]
    pos_dev = targets.shape[0]
    capacity = 2 * sub_dev // vocab_count
    slots = vocab_count * capacity
    out_pos = positions // vocab_count
    small = out_pos // CHUNKS
    rows = pos_dev // CHUNKS

    table_far = lax.ppermute(table, "core", SWAP)
    ordered = hidden.reshape(nx, nc, pos_dev // out_pos, CHUNKS, small, width)
    ordered = ordered.transpose(3, 0, 1, 2, 4, 5).reshape(CHUNKS, nx, nc, rows, width)
    far = lax.dynamic_index_in_dim(ordered, 1 - core, 2, keepdims=False)
    far = lax.ppermute(far, "core", SWAP)

    targets = targets.reshape(pos_dev // out_pos, CHUNKS, small, sub_dev)
    targets = targets.transpose(1, 0, 2, 3).reshape(pos_dev, sub_dev)
    slot_index, local_row = slots_of(subset_ids, owner_rows, vocab_count, capacity)
    to_slot = (jnp.arange(slots)[:, None] == slot_index[None, :]).astype(bf16)
    line = lax.broadcasted_iota(i32, (-pos_dev % 128 or 128, 1), 0)
    side = jnp.where(line == 0, local_row // LOW, jnp.where(line == 1, local_row % LOW, line == 2))
    sent = jnp.concatenate([targets, side.astype(bf16)], axis=0)
    payload = matmul(to_slot, sent, 1, 1, bf16)
    payload, far = lax.optimization_barrier((payload, far))
    got = lax.all_to_all(
        payload.reshape(vocab_count, capacity, -1), VOCAB, split_axis=0, concat_axis=0, tiled=True
    ).reshape(slots, -1)

    parts = []
    for c in range(CHUNKS):
        if c:
            far, parts[0][0] = lax.optimization_barrier((far, parts[0][0]))
        *codes, own = partial_logits(pos, ordered, far, table, table_far, c)
        parts.append(
            [own] + [lax.ppermute(codes[k - 1], "x", shift("x", k)) for k in (2, 1, 3)]
        )

    logits = [sum_codes(parts[0][0], parts[0][1:])]
    got, later, logits[0] = lax.optimization_barrier((got, ordered, logits[0]))
    info = got[:, pos_dev : pos_dev + 3].astype(i32)
    row_of = jnp.where(info[:, 2] > 0, info[:, 0] * LOW + info[:, 1], -1)
    to_row = (row_of[:, None] == jnp.arange(owner_rows)[None, :]).astype(bf16)
    landed = matmul(got, to_row, 0, 0)
    chosen = landed[pos_dev + 2 : pos_dev + 3] > 0.5

    order = [lax.dynamic_index_in_dim(later, (x + j) % nx, 1, False) for j in range(nx)]
    order = jnp.stack(order, 1)
    order = [lax.dynamic_index_in_dim(order, i, 2, False) for i in (core, 1 - core)]
    order = jnp.stack(order, 1).reshape(positions, width)
    order, *parts[1] = lax.optimization_barrier((order, *parts[1]))
    local = []
    for c in range(CHUNKS):
        if c:
            *parts[c], local[-1] = lax.optimization_barrier((*parts[c], local[-1]))
            logits.append(sum_codes(parts[c][0], parts[c][1:]))
        here = logits[c]
        peak = jnp.max(jnp.where(chosen, here, FAR), axis=1)
        total = jnp.sum(jnp.where(chosen, jnp.exp(here - peak[:, None]), 0.0), axis=1)
        local.append(jnp.stack([peak, total, jnp.sum(landed[c * rows : (c + 1) * rows], axis=1)]))
    stats = jnp.stack(local).reshape(1, CHUNKS * 3 * rows)
    stats = jnp.broadcast_to(stats, (vocab_count,) + stats.shape[1:])
    stats = lax.all_to_all(stats, VOCAB, split_axis=0, concat_axis=0, tiled=True)
    stats = stats.reshape(vocab_count, CHUNKS, 3, rows)
    row_peak = jnp.max(stats[:, :, 0], axis=0)
    row_total = jnp.sum(stats[:, :, 1] * jnp.exp(stats[:, :, 0] - row_peak[None]), axis=0)
    row_mass = jnp.sum(stats[:, :, 2], axis=0)
    mine = []
    for c in range(CHUNKS):
        probs = jnp.exp(logits[c] - row_peak[c][:, None]) / row_total[c][:, None]
        grad = LOSS_SCALE * (probs * row_mass[c][:, None] - landed[c * rows : (c + 1) * rows])
        mine.append(jnp.where(chosen, grad, 0.0).astype(bf16))
    mine = jnp.stack(mine)

    out = matmul(to_row, jnp.concatenate(logits, axis=0).astype(bf16), 1, 1, bf16)

    blocks = [lax.ppermute(mine, "x", shift("x", -j)) for j in range(1, nx)]
    back = lax.all_to_all(
        out.reshape(vocab_count, capacity, pos_dev), VOCAB, split_axis=0, concat_axis=0, tiled=True
    ).reshape(slots, pos_dev)
    stacked = stack_chunks([mine] + blocks)
    back, *stacked = lax.optimization_barrier((back, *stacked))
    pieces, terms = [], []
    for c, here in enumerate(stacked):
        there = lax.ppermute(here, "core", SWAP)
        terms += [here, there]
        if c:
            pieces[0][0], there = lax.optimization_barrier((pieces[0][0], there))
        *sent, own = hidden_parts(pos, (here, there), table, True)
        pieces.append(
            [own, [lax.ppermute(sent[k - 1], "y", shift("y", k)) for k in (2, 1, 3)]]
        )
    (pieces[0][0], pieces[1][0]) = lax.optimization_barrier((pieces[0][0], pieces[1][0]))
    first = add_and_code(*pieces[0], nz)
    first, terms[0] = lax.optimization_barrier((first, terms[0]))
    table_grad = matmul(jnp.concatenate(terms).reshape(positions, -1), order, 0, 0, bf16)
    pieces = [first, add_and_code(*pieces[1], nz, (table_grad,))]
    pieces = [lax.all_to_all(p, "z", split_axis=0, concat_axis=0, tiled=True) for p in pieces]
    pieces = [jnp.sum(decode(p), axis=0).astype(bf16) for p in pieces]
    hidden_grad = jnp.concatenate(pieces, axis=0)

    draft = matmul(back, to_slot, 0, 0, bf16)
    draft = draft.reshape(CHUNKS, pos_dev // out_pos, small, sub_dev).transpose(1, 0, 2, 3)
    return draft.reshape(pos_dev, sub_dev), hidden_grad, table_grad


def solution(mesh):
    fine = Mesh(mesh.devices.reshape(4, 2, 4, 8), ROWS + VOCAB)
    return jax.shard_map(
        on_device,
        mesh=fine,
        in_specs=(P(None, ROWS), P(VOCAB, ROWS), P(VOCAB), P(ROWS, VOCAB)),
        out_specs=(P(ROWS, VOCAB), P(VOCAB, ROWS), P(VOCAB, ROWS)),
        check_vma=False,
    )
```

```python
import functools

import jax
import jax.numpy as jnp
from jax import lax
from jax.experimental import pallas as pl
from jax.experimental.pallas import tpu as pltpu
from jax.sharding import Mesh, PartitionSpec as P

LOSS_SCALE = 32.0
LOW = 64
GROUP = 96
TILES = 4
HTILES = 4
FAR = -3.0e38
SIDE = 128
STACK = 10
CHUNKS = 2
ROWS = ("x", "core")
VOCAB = ("y", "z")
SMALL = 24 * 1024 * 1024
LARGE = 56 * 1024 * 1024
f32, bf16, i32, i16 = jnp.float32, jnp.bfloat16, jnp.int32, jnp.int16
SWAP = [(0, 1), (1, 0)]


def shift(axis, by):
    n = lax.axis_size(axis)
    return [(i, (i + by) % n) for i in range(n)]


def matmul(a, b, ca, cb, dtype=f32):
    return lax.dot_general(a, b, (((ca,), (cb,)), ((), ())), preferred_element_type=dtype)


def store_code(part, put):
    top = jnp.maximum(jnp.max(jnp.abs(part), axis=1, keepdims=True), 1e-30) * 1.0001
    power = jnp.ceil(jnp.log(top) * 1.4426950408889634) - 15.0
    code = jnp.round(part * jnp.exp2(-power)).astype(i32).astype(i16)
    width = part.shape[1]
    put(slice(0, width), code)
    side = jnp.broadcast_to(power, (part.shape[0], SIDE))
    put(slice(width, width + SIDE), side.astype(i32).astype(i16))


def decode(code):
    width = code.shape[-1] - SIDE
    return code[..., :width].astype(f32) * jnp.exp2(code[..., width : width + 1].astype(f32))


def code_rows(source, target):
    def body(r, _):
        span = pl.ds(pl.multiple_of(r * GROUP, GROUP), GROUP)

        def put(cols, value):
            target[span, cols] = value

        store_code(source(span), put)
        return 0

    lax.fori_loop(0, target.shape[0] // GROUP, body, 0)


def logits_kernel(nx, tile, pos, near, far, table, table_far, *refs):
    codes, (own, part) = refs[:-2], refs[-2:]
    step = pl.program_id(0)
    rows, width = near.shape[3:]
    columns = pl.ds(pl.multiple_of(step * tile, tile), tile)
    left = near[...].reshape(nx * rows, width)
    right = far[...].reshape(nx * rows, width)
    out = matmul(left, table[...], 1, 1) + matmul(right, table_far[...], 1, 1)
    part[:, :, columns] = out.reshape(nx, rows, tile)

    @pl.when(step == pl.num_programs(0) - 1)
    def _():
        x = pos[0]
        for k, code in enumerate(codes, 1):
            to = lax.rem(x + k, nx)
            code_rows(lambda span, to=to: part[to, span, :], code)
        own[...] = part[x]


def partial_logits(pos, near, far, table, table_far, chunk):
    _, nx, nc, rows, width = near.shape
    owner_rows = table.shape[0]
    tile = owner_rows // TILES
    return pl.pallas_call(
        functools.partial(logits_kernel, nx, tile),
        grid_spec=pltpu.PrefetchScalarGridSpec(
            num_scalar_prefetch=1,
            grid=(owner_rows // tile,),
            in_specs=[
                pl.BlockSpec((1, nx, 1, rows, width), lambda t, pos: (chunk, 0, pos[1], 0, 0)),
                pl.BlockSpec((1, nx, rows, width), lambda t, pos: (chunk, 0, 0, 0)),
                pl.BlockSpec((tile, width), lambda t, pos: (t, 0)),
                pl.BlockSpec((tile, width), lambda t, pos: (t, 0)),
            ],
            out_specs=[pl.BlockSpec((rows, owner_rows + SIDE), lambda t, pos: (0, 0))] * (nx - 1)
            + [pl.BlockSpec((rows, owner_rows), lambda t, pos: (0, 0))],
            scratch_shapes=[pltpu.VMEM((nx, rows, owner_rows), f32)],
        ),
        out_shape=[jax.ShapeDtypeStruct((rows, owner_rows + SIDE), i16)] * (nx - 1)
        + [jax.ShapeDtypeStruct((rows, owner_rows), f32)],
        compiler_params=pltpu.CompilerParams(vmem_limit_bytes=SMALL),
        cost_estimate=pl.CostEstimate(
            flops=12 * nx * rows * width * owner_rows, bytes_accessed=16 << 20, transcendentals=0
        ),
    )(pos, near, far, table, table_far)


def hidden_kernel(nx, tile, turned, pos, *refs):
    grads, table, codes, (own, part) = refs[: -nx - 2], refs[-nx - 2], refs[-nx - 1 : -2], refs[-2:]
    step = pl.program_id(0)
    x, core, y = pos[0], pos[1], pos[2]
    columns = pl.ds(pl.multiple_of(step * tile, tile), tile)
    for ref, where in zip(grads, (core, 1 - core)):
        rows = ref.shape[1]
        out = matmul(ref[...].reshape(nx * rows, -1), table[...], 1, 0)
        if not turned:
            part[:, :, columns] = out.reshape(nx, rows, tile)
            continue
        span = pl.ds(pl.multiple_of(where * rows, rows), rows)
        for j in range(nx):
            part[lax.rem(x + j, nx), span, columns] = out[j * rows : (j + 1) * rows]

    @pl.when(step == pl.num_programs(0) - 1)
    def _():
        for k, code in enumerate(codes, 1):
            to = lax.rem(y + k, nx)
            code_rows(lambda span, to=to: part[to, span, :], code)
        own[...] = part[y]


def hidden_parts(pos, grads, table, turned):
    nx, rows, owner_rows = grads[0].shape
    total = len(grads) * rows
    width = table.shape[1]
    tile = width // HTILES
    block = pl.BlockSpec((nx, rows, owner_rows), lambda t, pos: (0, 0, 0))
    return pl.pallas_call(
        functools.partial(hidden_kernel, nx, tile, turned),
        grid_spec=pltpu.PrefetchScalarGridSpec(
            num_scalar_prefetch=1,
            grid=(width // tile,),
            in_specs=[block] * len(grads)
            + [pl.BlockSpec((owner_rows, tile), lambda t, pos: (0, t))],
            out_specs=[pl.BlockSpec((total, width + SIDE), lambda t, pos: (0, 0))] * (nx - 1)
            + [pl.BlockSpec((total, width), lambda t, pos: (0, 0))],
            scratch_shapes=[pltpu.VMEM((nx, total, width), f32)],
        ),
        out_shape=[jax.ShapeDtypeStruct((total, width + SIDE), i16)] * (nx - 1)
        + [jax.ShapeDtypeStruct((total, width), f32)],
        compiler_params=pltpu.CompilerParams(vmem_limit_bytes=SMALL),
        cost_estimate=pl.CostEstimate(
            flops=10 << 30, bytes_accessed=8 << 20, transcendentals=0
        ),
    )(pos, *grads, table)


def add_kernel(own, a, b, c, *rest):
    code = rest[-1]
    part = own[...]
    for ref in (a, b, c):
        part = part + decode(ref[...])

    def put(cols, value):
        code[:, :, cols] = value.reshape(code.shape[0], code.shape[1], -1)

    store_code(part, put)


def add_and_code(own, arrived, pieces, after=()):
    rows, width = own.shape
    whole = pl.BlockSpec(memory_space=pltpu.VMEM)
    return pl.pallas_call(
        add_kernel,
        in_specs=[whole] * 4 + [pl.BlockSpec(memory_space=pl.ANY)] * len(after),
        out_specs=whole,
        out_shape=jax.ShapeDtypeStruct((pieces, rows // pieces, width + SIDE), i16),
        compiler_params=pltpu.CompilerParams(vmem_limit_bytes=LARGE),
        cost_estimate=pl.CostEstimate(flops=12 << 30, bytes_accessed=8 << 20, transcendentals=0),
    )(own, *arrived, *after)


def sum_kernel(own, a, b, c, out):
    total = own[...]
    for ref in (a, b, c):
        total = total + decode(ref[...])
    out[...] = total


def sum_codes(own, arrived):
    return pl.pallas_call(
        sum_kernel,
        out_shape=jax.ShapeDtypeStruct(own.shape, f32),
        compiler_params=pltpu.CompilerParams(vmem_limit_bytes=SMALL),
        cost_estimate=pl.CostEstimate(flops=12 << 30, bytes_accessed=4 << 20, transcendentals=0),
    )(own, *arrived)


def stack_kernel(*refs):
    count = len(refs) - CHUNKS
    for c, out in enumerate(refs[count:]):
        for j in range(count):
            out[j] = refs[j][c]


def stack_chunks(blocks):
    _, rows, width = blocks[0].shape
    return pl.pallas_call(
        stack_kernel,
        out_shape=[jax.ShapeDtypeStruct((len(blocks), rows, width), bf16)] * CHUNKS,
        compiler_params=pltpu.CompilerParams(vmem_limit_bytes=LARGE),
        cost_estimate=pl.CostEstimate(flops=STACK << 30, bytes_accessed=6 << 20, transcendentals=0),
    )(*blocks)


def slots_of(subset_ids, owner_rows, vocab_count, capacity):
    count = subset_ids.shape[0]
    owner_of = subset_ids // owner_rows
    onehot = (owner_of[:, None] == jnp.arange(vocab_count)[None, :]).astype(bf16)
    earlier = (jnp.arange(count)[:, None] > jnp.arange(count)[None, :]).astype(bf16)
    before = matmul(earlier, onehot, 1, 0)
    rank = jnp.sum(before * onehot.astype(f32), axis=1).astype(i32)
    return owner_of * capacity + rank, subset_ids % owner_rows


def on_device(hidden, table, subset_ids, targets):
    nx, nc, ny, nz = (lax.axis_size(a) for a in ("x", "core", "y", "z"))
    x, core, y = (lax.axis_index(a) for a in ("x", "core", "y"))
    pos = jnp.stack([x, core, y]).astype(i32)
    vocab_count = ny * nz
    positions, width = hidden.shape
    owner_rows = table.shape[0]
    sub_dev = subset_ids.shape[0]
    pos_dev = targets.shape[0]
    capacity = 2 * sub_dev // vocab_count
    slots = vocab_count * capacity
    out_pos = positions // vocab_count
    small = out_pos // CHUNKS
    rows = pos_dev // CHUNKS

    table_far = lax.ppermute(table, "core", SWAP)
    ordered = hidden.reshape(nx, nc, pos_dev // out_pos, CHUNKS, small, width)
    ordered = ordered.transpose(3, 0, 1, 2, 4, 5).reshape(CHUNKS, nx, nc, rows, width)
    far = lax.dynamic_index_in_dim(ordered, 1 - core, 2, keepdims=False)
    far = lax.ppermute(far, "core", SWAP)

    targets = targets.reshape(pos_dev // out_pos, CHUNKS, small, sub_dev)
    targets = targets.transpose(1, 0, 2, 3).reshape(pos_dev, sub_dev)
    slot_index, local_row = slots_of(subset_ids, owner_rows, vocab_count, capacity)
    to_slot = (jnp.arange(slots)[:, None] == slot_index[None, :]).astype(bf16)
    line = lax.broadcasted_iota(i32, (-pos_dev % 128 or 128, 1), 0)
    side = jnp.where(line == 0, local_row // LOW, jnp.where(line == 1, local_row % LOW, line == 2))
    sent = jnp.concatenate([targets, side.astype(bf16)], axis=0)
    payload = matmul(to_slot, sent, 1, 1, bf16)
    payload, far = lax.optimization_barrier((payload, far))
    got = lax.all_to_all(
        payload.reshape(vocab_count, capacity, -1), VOCAB, split_axis=0, concat_axis=0, tiled=True
    ).reshape(slots, -1)

    parts = []
    for c in range(CHUNKS):
        if c:
            far, parts[0][0] = lax.optimization_barrier((far, parts[0][0]))
        *codes, own = partial_logits(pos, ordered, far, table, table_far, c)
        parts.append(
            [own] + [lax.ppermute(codes[k - 1], "x", shift("x", k)) for k in (2, 1, 3)]
        )

    logits = [sum_codes(parts[0][0], parts[0][1:])]
    got, later, logits[0] = lax.optimization_barrier((got, ordered, logits[0]))
    info = got[:, pos_dev : pos_dev + 3].astype(i32)
    row_of = jnp.where(info[:, 2] > 0, info[:, 0] * LOW + info[:, 1], -1)
    to_row = (row_of[:, None] == jnp.arange(owner_rows)[None, :]).astype(bf16)
    landed = matmul(got, to_row, 0, 0)
    chosen = landed[pos_dev + 2 : pos_dev + 3] > 0.5

    order = [lax.dynamic_index_in_dim(later, (x + j) % nx, 1, False) for j in range(nx)]
    order = jnp.stack(order, 1)
    order = [lax.dynamic_index_in_dim(order, i, 2, False) for i in (core, 1 - core)]
    order = jnp.stack(order, 1).reshape(positions, width)
    order, *parts[1] = lax.optimization_barrier((order, *parts[1]))
    local = []
    for c in range(CHUNKS):
        if c:
            *parts[c], local[-1] = lax.optimization_barrier((*parts[c], local[-1]))
            logits.append(sum_codes(parts[c][0], parts[c][1:]))
        here = logits[c]
        peak = jnp.max(jnp.where(chosen, here, FAR), axis=1)
        total = jnp.sum(jnp.where(chosen, jnp.exp(here - peak[:, None]), 0.0), axis=1)
        local.append(jnp.stack([peak, total, jnp.sum(landed[c * rows : (c + 1) * rows], axis=1)]))
    stats = jnp.stack(local).reshape(1, CHUNKS * 3 * rows)
    stats = jnp.broadcast_to(stats, (vocab_count,) + stats.shape[1:])
    stats = lax.all_to_all(stats, VOCAB, split_axis=0, concat_axis=0, tiled=True)
    stats = stats.reshape(vocab_count, CHUNKS, 3, rows)
    row_peak = jnp.max(stats[:, :, 0], axis=0)
    row_total = jnp.sum(stats[:, :, 1] * jnp.exp(stats[:, :, 0] - row_peak[None]), axis=0)
    row_mass = jnp.sum(stats[:, :, 2], axis=0)
    mine = []
    for c in range(CHUNKS):
        probs = jnp.exp(logits[c] - row_peak[c][:, None]) / row_total[c][:, None]
        grad = LOSS_SCALE * (probs * row_mass[c][:, None] - landed[c * rows : (c + 1) * rows])
        mine.append(jnp.where(chosen, grad, 0.0).astype(bf16))
    mine = jnp.stack(mine)

    out = matmul(to_row, jnp.concatenate(logits, axis=0).astype(bf16), 1, 1, bf16)

    blocks = [lax.ppermute(mine, "x", shift("x", -j)) for j in range(1, nx)]
    back = lax.all_to_all(
        out.reshape(vocab_count, capacity, pos_dev), VOCAB, split_axis=0, concat_axis=0, tiled=True
    ).reshape(slots, pos_dev)
    stacked = stack_chunks([mine] + blocks)
    back, *stacked = lax.optimization_barrier((back, *stacked))
    pieces, terms = [], []
    for c, here in enumerate(stacked):
        there = lax.ppermute(here, "core", SWAP)
        terms += [here, there]
        if c:
            pieces[0][0], there = lax.optimization_barrier((pieces[0][0], there))
        *sent, own = hidden_parts(pos, (here, there), table, True)
        pieces.append(
            [own, [lax.ppermute(sent[k - 1], "y", shift("y", k)) for k in (2, 1, 3)]]
        )
    (pieces[0][0], pieces[1][0]) = lax.optimization_barrier((pieces[0][0], pieces[1][0]))
    first = add_and_code(*pieces[0], nz)
    first, terms[0] = lax.optimization_barrier((first, terms[0]))
    table_grad = matmul(jnp.concatenate(terms).reshape(positions, -1), order, 0, 0, bf16)
    pieces = [first, add_and_code(*pieces[1], nz, (table_grad,))]
    pieces = [lax.all_to_all(p, "z", split_axis=0, concat_axis=0, tiled=True) for p in pieces]
    pieces = [jnp.sum(decode(p), axis=0).astype(bf16) for p in pieces]
    hidden_grad = jnp.concatenate(pieces, axis=0)

    draft = matmul(back, to_slot, 0, 0, bf16)
    draft = draft.reshape(CHUNKS, pos_dev // out_pos, small, sub_dev).transpose(1, 0, 2, 3)
    return draft.reshape(pos_dev, sub_dev), hidden_grad, table_grad


def solution(mesh):
    fine = Mesh(mesh.devices.reshape(4, 2, 4, 8), ROWS + VOCAB)
    return jax.shard_map(
        on_device,
        mesh=fine,
        in_specs=(P(None, ROWS), P(VOCAB, ROWS), P(VOCAB), P(ROWS, VOCAB)),
        out_specs=(P(ROWS, VOCAB), P(VOCAB, ROWS), P(VOCAB, ROWS)),
        check_vma=False,
    )
```

```python
import functools

import jax
import jax.numpy as jnp
from jax import lax
from jax.experimental import pallas as pl
from jax.experimental.pallas import tpu as pltpu
from jax.sharding import Mesh, PartitionSpec as P

LOSS_SCALE = 32.0
LOW = 64
GROUP = 96
TILES = 4
HTILES = 4
FAR = -3.0e38
SIDE = 128
STACK = 10
CHUNKS = 2
ROWS = ("x", "core")
VOCAB = ("y", "z")
SMALL = 24 * 1024 * 1024
LARGE = 56 * 1024 * 1024
f32, bf16, i32, i16 = jnp.float32, jnp.bfloat16, jnp.int32, jnp.int16
SWAP = [(0, 1), (1, 0)]


def shift(axis, by):
    n = lax.axis_size(axis)
    return [(i, (i + by) % n) for i in range(n)]


def matmul(a, b, ca, cb, dtype=f32):
    return lax.dot_general(a, b, (((ca,), (cb,)), ((), ())), preferred_element_type=dtype)


def store_code(part, put):
    top = jnp.maximum(jnp.max(jnp.abs(part), axis=1, keepdims=True), 1e-30) * 1.0001
    power = jnp.ceil(jnp.log(top) * 1.4426950408889634) - 15.0
    code = jnp.round(part * jnp.exp2(-power)).astype(i32).astype(i16)
    width = part.shape[1]
    put(slice(0, width), code)
    side = jnp.broadcast_to(power, (part.shape[0], SIDE))
    put(slice(width, width + SIDE), side.astype(i32).astype(i16))


def decode(code):
    width = code.shape[-1] - SIDE
    return code[..., :width].astype(f32) * jnp.exp2(code[..., width : width + 1].astype(f32))


def code_rows(source, target):
    def body(r, _):
        span = pl.ds(pl.multiple_of(r * GROUP, GROUP), GROUP)

        def put(cols, value):
            target[span, cols] = value

        store_code(source(span), put)
        return 0

    lax.fori_loop(0, target.shape[0] // GROUP, body, 0)


def logits_kernel(nx, tile, pos, near, far, table, table_far, *refs):
    codes, (own, part) = refs[:-2], refs[-2:]
    step = pl.program_id(0)
    rows, width = near.shape[3:]
    columns = pl.ds(pl.multiple_of(step * tile, tile), tile)
    left = near[...].reshape(nx * rows, width)
    right = far[...].reshape(nx * rows, width)
    out = matmul(left, table[...], 1, 1) + matmul(right, table_far[...], 1, 1)
    part[:, :, columns] = out.reshape(nx, rows, tile)

    @pl.when(step == pl.num_programs(0) - 1)
    def _():
        x = pos[0]
        for k, code in enumerate(codes, 1):
            to = lax.rem(x + k, nx)
            code_rows(lambda span, to=to: part[to, span, :], code)
        own[...] = part[x]


def partial_logits(pos, near, far, table, table_far, chunk):
    _, nx, nc, rows, width = near.shape
    owner_rows = table.shape[0]
    tile = owner_rows // TILES
    return pl.pallas_call(
        functools.partial(logits_kernel, nx, tile),
        grid_spec=pltpu.PrefetchScalarGridSpec(
            num_scalar_prefetch=1,
            grid=(owner_rows // tile,),
            in_specs=[
                pl.BlockSpec((1, nx, 1, rows, width), lambda t, pos: (chunk, 0, pos[1], 0, 0)),
                pl.BlockSpec((1, nx, rows, width), lambda t, pos: (chunk, 0, 0, 0)),
                pl.BlockSpec((tile, width), lambda t, pos: (t, 0)),
                pl.BlockSpec((tile, width), lambda t, pos: (t, 0)),
            ],
            out_specs=[pl.BlockSpec((rows, owner_rows + SIDE), lambda t, pos: (0, 0))] * (nx - 1)
            + [pl.BlockSpec((rows, owner_rows), lambda t, pos: (0, 0))],
            scratch_shapes=[pltpu.VMEM((nx, rows, owner_rows), f32)],
        ),
        out_shape=[jax.ShapeDtypeStruct((rows, owner_rows + SIDE), i16)] * (nx - 1)
        + [jax.ShapeDtypeStruct((rows, owner_rows), f32)],
        compiler_params=pltpu.CompilerParams(vmem_limit_bytes=SMALL),
        cost_estimate=pl.CostEstimate(
            flops=12 * nx * rows * width * owner_rows, bytes_accessed=16 << 20, transcendentals=0
        ),
    )(pos, near, far, table, table_far)


def hidden_kernel(nx, tile, turned, pos, *refs):
    grads, table, codes, (own, part) = refs[: -nx - 2], refs[-nx - 2], refs[-nx - 1 : -2], refs[-2:]
    step = pl.program_id(0)
    x, core, y = pos[0], pos[1], pos[2]
    columns = pl.ds(pl.multiple_of(step * tile, tile), tile)
    for ref, where in zip(grads, (core, 1 - core)):
        rows = ref.shape[1]
        out = matmul(ref[...].reshape(nx * rows, -1), table[...], 1, 0)
        if not turned:
            part[:, :, columns] = out.reshape(nx, rows, tile)
            continue
        span = pl.ds(pl.multiple_of(where * rows, rows), rows)
        for j in range(nx):
            part[lax.rem(x + j, nx), span, columns] = out[j * rows : (j + 1) * rows]

    @pl.when(step == pl.num_programs(0) - 1)
    def _():
        for k, code in enumerate(codes, 1):
            to = lax.rem(y + k, nx)
            code_rows(lambda span, to=to: part[to, span, :], code)
        own[...] = part[y]


def hidden_parts(pos, grads, table, turned):
    nx, rows, owner_rows = grads[0].shape
    total = len(grads) * rows
    width = table.shape[1]
    tile = width // HTILES
    block = pl.BlockSpec((nx, rows, owner_rows), lambda t, pos: (0, 0, 0))
    return pl.pallas_call(
        functools.partial(hidden_kernel, nx, tile, turned),
        grid_spec=pltpu.PrefetchScalarGridSpec(
            num_scalar_prefetch=1,
            grid=(width // tile,),
            in_specs=[block] * len(grads)
            + [pl.BlockSpec((owner_rows, tile), lambda t, pos: (0, t))],
            out_specs=[pl.BlockSpec((total, width + SIDE), lambda t, pos: (0, 0))] * (nx - 1)
            + [pl.BlockSpec((total, width), lambda t, pos: (0, 0))],
            scratch_shapes=[pltpu.VMEM((nx, total, width), f32)],
        ),
        out_shape=[jax.ShapeDtypeStruct((total, width + SIDE), i16)] * (nx - 1)
        + [jax.ShapeDtypeStruct((total, width), f32)],
        compiler_params=pltpu.CompilerParams(vmem_limit_bytes=SMALL),
        cost_estimate=pl.CostEstimate(
            flops=10 << 30, bytes_accessed=8 << 20, transcendentals=0
        ),
    )(pos, *grads, table)


def add_kernel(own, a, b, c, *rest):
    code = rest[-1]
    part = own[...]
    for ref in (a, b, c):
        part = part + decode(ref[...])

    def put(cols, value):
        code[:, :, cols] = value.reshape(code.shape[0], code.shape[1], -1)

    store_code(part, put)


def add_and_code(own, arrived, pieces, after=()):
    rows, width = own.shape
    whole = pl.BlockSpec(memory_space=pltpu.VMEM)
    return pl.pallas_call(
        add_kernel,
        in_specs=[whole] * 4 + [pl.BlockSpec(memory_space=pl.ANY)] * len(after),
        out_specs=whole,
        out_shape=jax.ShapeDtypeStruct((pieces, rows // pieces, width + SIDE), i16),
        compiler_params=pltpu.CompilerParams(vmem_limit_bytes=LARGE),
        cost_estimate=pl.CostEstimate(flops=12 << 30, bytes_accessed=8 << 20, transcendentals=0),
    )(own, *arrived, *after)


def sum_kernel(own, a, b, c, out):
    total = own[...]
    for ref in (a, b, c):
        total = total + decode(ref[...])
    out[...] = total


def sum_codes(own, arrived):
    return pl.pallas_call(
        sum_kernel,
        out_shape=jax.ShapeDtypeStruct(own.shape, f32),
        compiler_params=pltpu.CompilerParams(vmem_limit_bytes=SMALL),
        cost_estimate=pl.CostEstimate(flops=12 << 30, bytes_accessed=4 << 20, transcendentals=0),
    )(own, *arrived)


def stack_kernel(mine, right, first, second, left, *outs):
    for c, (out, across) in enumerate(zip(outs, (first, second))):
        out[0] = mine[c]
        out[1] = right[c]
        out[2] = across[...]
        out[3] = left[c]


def stack_chunks(mine, right, passed, left):
    _, rows, width = mine.shape
    return pl.pallas_call(
        stack_kernel,
        out_shape=[jax.ShapeDtypeStruct((4, rows, width), bf16)] * CHUNKS,
        compiler_params=pltpu.CompilerParams(vmem_limit_bytes=LARGE),
        cost_estimate=pl.CostEstimate(flops=STACK << 30, bytes_accessed=6 << 20, transcendentals=0),
    )(mine, right, *passed, left)


def slots_of(subset_ids, owner_rows, vocab_count, capacity):
    count = subset_ids.shape[0]
    owner_of = subset_ids // owner_rows
    onehot = (owner_of[:, None] == jnp.arange(vocab_count)[None, :]).astype(bf16)
    earlier = (jnp.arange(count)[:, None] > jnp.arange(count)[None, :]).astype(bf16)
    before = matmul(earlier, onehot, 1, 0)
    rank = jnp.sum(before * onehot.astype(f32), axis=1).astype(i32)
    return owner_of * capacity + rank, subset_ids % owner_rows


def on_device(hidden, table, subset_ids, targets):
    nx, nc, ny, nz = (lax.axis_size(a) for a in ("x", "core", "y", "z"))
    x, core, y = (lax.axis_index(a) for a in ("x", "core", "y"))
    pos = jnp.stack([x, core, y]).astype(i32)
    vocab_count = ny * nz
    positions, width = hidden.shape
    owner_rows = table.shape[0]
    sub_dev = subset_ids.shape[0]
    pos_dev = targets.shape[0]
    capacity = 2 * sub_dev // vocab_count
    slots = vocab_count * capacity
    out_pos = positions // vocab_count
    small = out_pos // CHUNKS
    rows = pos_dev // CHUNKS

    table_far = lax.ppermute(table, "core", SWAP)
    ordered = hidden.reshape(nx, nc, pos_dev // out_pos, CHUNKS, small, width)
    ordered = ordered.transpose(3, 0, 1, 2, 4, 5).reshape(CHUNKS, nx, nc, rows, width)
    far = lax.dynamic_index_in_dim(ordered, 1 - core, 2, keepdims=False)
    far = lax.ppermute(far, "core", SWAP)

    targets = targets.reshape(pos_dev // out_pos, CHUNKS, small, sub_dev)
    targets = targets.transpose(1, 0, 2, 3).reshape(pos_dev, sub_dev)
    slot_index, local_row = slots_of(subset_ids, owner_rows, vocab_count, capacity)
    to_slot = (jnp.arange(slots)[:, None] == slot_index[None, :]).astype(bf16)
    line = lax.broadcasted_iota(i32, (-pos_dev % 128 or 128, 1), 0)
    side = jnp.where(line == 0, local_row // LOW, jnp.where(line == 1, local_row % LOW, line == 2))
    sent = jnp.concatenate([targets, side.astype(bf16)], axis=0)
    payload = matmul(to_slot, sent, 1, 1, bf16)
    payload, far = lax.optimization_barrier((payload, far))
    got = lax.all_to_all(
        payload.reshape(vocab_count, capacity, -1), VOCAB, split_axis=0, concat_axis=0, tiled=True
    ).reshape(slots, -1)

    parts = []
    for c in range(CHUNKS):
        if c:
            far, parts[0][0] = lax.optimization_barrier((far, parts[0][0]))
        *codes, own = partial_logits(pos, ordered, far, table, table_far, c)
        parts.append(
            [own] + [lax.ppermute(codes[k - 1], "x", shift("x", k)) for k in (2, 1, 3)]
        )

    logits = [sum_codes(parts[0][0], parts[0][1:])]
    got, later, logits[0] = lax.optimization_barrier((got, ordered, logits[0]))
    info = got[:, pos_dev : pos_dev + 3].astype(i32)
    row_of = jnp.where(info[:, 2] > 0, info[:, 0] * LOW + info[:, 1], -1)
    to_row = (row_of[:, None] == jnp.arange(owner_rows)[None, :]).astype(bf16)
    landed = matmul(got, to_row, 0, 0)
    chosen = landed[pos_dev + 2 : pos_dev + 3] > 0.5

    order = [lax.dynamic_index_in_dim(later, (x + j) % nx, 1, False) for j in range(nx)]
    order = jnp.stack(order, 1)
    order = [lax.dynamic_index_in_dim(order, i, 2, False) for i in (core, 1 - core)]
    order = jnp.stack(order, 1).reshape(positions, width)
    order, *parts[1] = lax.optimization_barrier((order, *parts[1]))
    local = []
    for c in range(CHUNKS):
        if c:
            *parts[c], local[-1] = lax.optimization_barrier((*parts[c], local[-1]))
            logits.append(sum_codes(parts[c][0], parts[c][1:]))
        here = logits[c]
        peak = jnp.max(jnp.where(chosen, here, FAR), axis=1)
        total = jnp.sum(jnp.where(chosen, jnp.exp(here - peak[:, None]), 0.0), axis=1)
        local.append(jnp.stack([peak, total, jnp.sum(landed[c * rows : (c + 1) * rows], axis=1)]))
    stats = jnp.stack(local).reshape(1, CHUNKS * 3 * rows)
    stats = jnp.broadcast_to(stats, (vocab_count,) + stats.shape[1:])
    stats = lax.all_to_all(stats, VOCAB, split_axis=0, concat_axis=0, tiled=True)
    stats = stats.reshape(vocab_count, CHUNKS, 3, rows)
    row_peak = jnp.max(stats[:, :, 0], axis=0)
    row_total = jnp.sum(stats[:, :, 1] * jnp.exp(stats[:, :, 0] - row_peak[None]), axis=0)
    row_mass = jnp.sum(stats[:, :, 2], axis=0)
    mine = []
    for c in range(CHUNKS):
        probs = jnp.exp(logits[c] - row_peak[c][:, None]) / row_total[c][:, None]
        grad = LOSS_SCALE * (probs * row_mass[c][:, None] - landed[c * rows : (c + 1) * rows])
        mine.append(jnp.where(chosen, grad, 0.0).astype(bf16))
    mine = jnp.stack(mine)

    out = matmul(to_row, jnp.concatenate(logits, axis=0).astype(bf16), 1, 1, bf16)

    right = lax.ppermute(mine, "x", shift("x", -1))
    left = lax.ppermute(mine, "x", shift("x", 1))
    passed = [
        lax.ppermute(right[0], "x", shift("x", -1)),
        lax.ppermute(left[1], "x", shift("x", 1)),
    ]
    back = lax.all_to_all(
        out.reshape(vocab_count, capacity, pos_dev), VOCAB, split_axis=0, concat_axis=0, tiled=True
    ).reshape(slots, pos_dev)
    stacked = stack_chunks(mine, right, passed, left)
    back, *stacked = lax.optimization_barrier((back, *stacked))
    pieces, terms = [], []
    for c, here in enumerate(stacked):
        there = lax.ppermute(here, "core", SWAP)
        terms += [here, there]
        if c:
            pieces[0][0], there = lax.optimization_barrier((pieces[0][0], there))
        *sent, own = hidden_parts(pos, (here, there), table, True)
        pieces.append(
            [own, [lax.ppermute(sent[k - 1], "y", shift("y", k)) for k in (2, 1, 3)]]
        )
    (pieces[0][0], pieces[1][0]) = lax.optimization_barrier((pieces[0][0], pieces[1][0]))
    first = add_and_code(*pieces[0], nz)
    first, terms[0] = lax.optimization_barrier((first, terms[0]))
    table_grad = matmul(jnp.concatenate(terms).reshape(positions, -1), order, 0, 0, bf16)
    pieces = [first, add_and_code(*pieces[1], nz, (table_grad,))]
    pieces = [lax.all_to_all(p, "z", split_axis=0, concat_axis=0, tiled=True) for p in pieces]
    pieces = [jnp.sum(decode(p), axis=0).astype(bf16) for p in pieces]
    hidden_grad = jnp.concatenate(pieces, axis=0)

    draft = matmul(back, to_slot, 0, 0, bf16)
    draft = draft.reshape(CHUNKS, pos_dev // out_pos, small, sub_dev).transpose(1, 0, 2, 3)
    return draft.reshape(pos_dev, sub_dev), hidden_grad, table_grad


def solution(mesh):
    fine = Mesh(mesh.devices.reshape(4, 2, 4, 8), ROWS + VOCAB)
    return jax.shard_map(
        on_device,
        mesh=fine,
        in_specs=(P(None, ROWS), P(VOCAB, ROWS), P(VOCAB), P(ROWS, VOCAB)),
        out_specs=(P(ROWS, VOCAB), P(VOCAB, ROWS), P(VOCAB, ROWS)),
        check_vma=False,
    )
```

```python
import functools

import jax
import jax.numpy as jnp
from jax import lax
from jax.experimental import pallas as pl
from jax.experimental.pallas import tpu as pltpu
from jax.sharding import Mesh, PartitionSpec as P

LOSS_SCALE = 32.0
LOW = 64
GROUP = 96
TILES = 4
HTILES = 4
FAR = -3.0e38
SIDE = 128
STACK = 10
CHUNKS = 2
ROWS = ("x", "core")
VOCAB = ("y", "z")
SMALL = 24 * 1024 * 1024
LARGE = 56 * 1024 * 1024
f32, bf16, i32, i16 = jnp.float32, jnp.bfloat16, jnp.int32, jnp.int16
SWAP = [(0, 1), (1, 0)]


def shift(axis, by):
    n = lax.axis_size(axis)
    return [(i, (i + by) % n) for i in range(n)]


def matmul(a, b, ca, cb, dtype=f32):
    return lax.dot_general(a, b, (((ca,), (cb,)), ((), ())), preferred_element_type=dtype)


def store_code(part, put):
    top = jnp.maximum(jnp.max(jnp.abs(part), axis=1, keepdims=True), 1e-30) * 1.0001
    power = jnp.ceil(jnp.log(top) * 1.4426950408889634) - 15.0
    code = jnp.round(part * jnp.exp2(-power)).astype(i32).astype(i16)
    width = part.shape[1]
    put(slice(0, width), code)
    side = jnp.broadcast_to(power, (part.shape[0], SIDE))
    put(slice(width, width + SIDE), side.astype(i32).astype(i16))


def decode(code):
    width = code.shape[-1] - SIDE
    return code[..., :width].astype(f32) * jnp.exp2(code[..., width : width + 1].astype(f32))


def code_rows(source, target):
    def body(r, _):
        span = pl.ds(pl.multiple_of(r * GROUP, GROUP), GROUP)

        def put(cols, value):
            target[span, cols] = value

        store_code(source(span), put)
        return 0

    lax.fori_loop(0, target.shape[0] // GROUP, body, 0)


def logits_kernel(nx, tile, pos, near, far, table, table_far, *refs):
    codes, (own, part) = refs[:-2], refs[-2:]
    step = pl.program_id(0)
    rows, width = near.shape[3:]
    columns = pl.ds(pl.multiple_of(step * tile, tile), tile)
    left = near[...].reshape(nx * rows, width)
    right = far[...].reshape(nx * rows, width)
    out = matmul(left, table[...], 1, 1) + matmul(right, table_far[...], 1, 1)
    part[:, :, columns] = out.reshape(nx, rows, tile)

    @pl.when(step == pl.num_programs(0) - 1)
    def _():
        x = pos[0]
        for k, code in enumerate(codes, 1):
            to = lax.rem(x + k, nx)
            code_rows(lambda span, to=to: part[to, span, :], code)
        own[...] = part[x]


def partial_logits(pos, near, far, table, table_far, chunk):
    _, nx, nc, rows, width = near.shape
    owner_rows = table.shape[0]
    tile = owner_rows // TILES
    return pl.pallas_call(
        functools.partial(logits_kernel, nx, tile),
        grid_spec=pltpu.PrefetchScalarGridSpec(
            num_scalar_prefetch=1,
            grid=(owner_rows // tile,),
            in_specs=[
                pl.BlockSpec((1, nx, 1, rows, width), lambda t, pos: (chunk, 0, pos[1], 0, 0)),
                pl.BlockSpec((1, nx, rows, width), lambda t, pos: (chunk, 0, 0, 0)),
                pl.BlockSpec((tile, width), lambda t, pos: (t, 0)),
                pl.BlockSpec((tile, width), lambda t, pos: (t, 0)),
            ],
            out_specs=[pl.BlockSpec((rows, owner_rows + SIDE), lambda t, pos: (0, 0))] * (nx - 1)
            + [pl.BlockSpec((rows, owner_rows), lambda t, pos: (0, 0))],
            scratch_shapes=[pltpu.VMEM((nx, rows, owner_rows), f32)],
        ),
        out_shape=[jax.ShapeDtypeStruct((rows, owner_rows + SIDE), i16)] * (nx - 1)
        + [jax.ShapeDtypeStruct((rows, owner_rows), f32)],
        compiler_params=pltpu.CompilerParams(vmem_limit_bytes=SMALL),
        cost_estimate=pl.CostEstimate(
            flops=12 * nx * rows * width * owner_rows, bytes_accessed=16 << 20, transcendentals=0
        ),
    )(pos, near, far, table, table_far)


def hidden_kernel(nx, tile, turned, pos, *refs):
    grads, table, codes, (own, part) = refs[: -nx - 2], refs[-nx - 2], refs[-nx - 1 : -2], refs[-2:]
    step = pl.program_id(0)
    x, core, y = pos[0], pos[1], pos[2]
    columns = pl.ds(pl.multiple_of(step * tile, tile), tile)
    for ref, where in zip(grads, (core, 1 - core)):
        rows = ref.shape[1]
        out = matmul(ref[...].reshape(nx * rows, -1), table[...], 1, 0)
        if not turned:
            part[:, :, columns] = out.reshape(nx, rows, tile)
            continue
        span = pl.ds(pl.multiple_of(where * rows, rows), rows)
        for j in range(nx):
            part[lax.rem(x + j, nx), span, columns] = out[j * rows : (j + 1) * rows]

    @pl.when(step == pl.num_programs(0) - 1)
    def _():
        for k, code in enumerate(codes, 1):
            to = lax.rem(y + k, nx)
            code_rows(lambda span, to=to: part[to, span, :], code)
        own[...] = part[y]


def hidden_parts(pos, grads, table, turned):
    nx, rows, owner_rows = grads[0].shape
    total = len(grads) * rows
    width = table.shape[1]
    tile = width // HTILES
    block = pl.BlockSpec((nx, rows, owner_rows), lambda t, pos: (0, 0, 0))
    return pl.pallas_call(
        functools.partial(hidden_kernel, nx, tile, turned),
        grid_spec=pltpu.PrefetchScalarGridSpec(
            num_scalar_prefetch=1,
            grid=(width // tile,),
            in_specs=[block] * len(grads)
            + [pl.BlockSpec((owner_rows, tile), lambda t, pos: (0, t))],
            out_specs=[pl.BlockSpec((total, width + SIDE), lambda t, pos: (0, 0))] * (nx - 1)
            + [pl.BlockSpec((total, width), lambda t, pos: (0, 0))],
            scratch_shapes=[pltpu.VMEM((nx, total, width), f32)],
        ),
        out_shape=[jax.ShapeDtypeStruct((total, width + SIDE), i16)] * (nx - 1)
        + [jax.ShapeDtypeStruct((total, width), f32)],
        compiler_params=pltpu.CompilerParams(vmem_limit_bytes=SMALL),
        cost_estimate=pl.CostEstimate(
            flops=10 << 30, bytes_accessed=8 << 20, transcendentals=0
        ),
    )(pos, *grads, table)


def add_kernel(own, a, b, c, *rest):
    code = rest[-1]
    part = own[...]
    for ref in (a, b, c):
        part = part + decode(ref[...])

    def put(cols, value):
        code[:, :, cols] = value.reshape(code.shape[0], code.shape[1], -1)

    store_code(part, put)


def add_and_code(own, arrived, pieces, after=()):
    rows, width = own.shape
    whole = pl.BlockSpec(memory_space=pltpu.VMEM)
    return pl.pallas_call(
        add_kernel,
        in_specs=[whole] * 4 + [pl.BlockSpec(memory_space=pl.ANY)] * len(after),
        out_specs=whole,
        out_shape=jax.ShapeDtypeStruct((pieces, rows // pieces, width + SIDE), i16),
        compiler_params=pltpu.CompilerParams(vmem_limit_bytes=LARGE),
        cost_estimate=pl.CostEstimate(flops=12 << 30, bytes_accessed=8 << 20, transcendentals=0),
    )(own, *arrived, *after)


def sum_kernel(own, a, b, c, out):
    total = own[...]
    for ref in (a, b, c):
        total = total + decode(ref[...])
    out[...] = total


def sum_codes(own, arrived):
    return pl.pallas_call(
        sum_kernel,
        out_shape=jax.ShapeDtypeStruct(own.shape, f32),
        compiler_params=pltpu.CompilerParams(vmem_limit_bytes=SMALL),
        cost_estimate=pl.CostEstimate(flops=12 << 30, bytes_accessed=4 << 20, transcendentals=0),
    )(own, *arrived)


def stack_kernel(mine, right, first, second, left, *outs):
    for c, (out, across) in enumerate(zip(outs, (first, second))):
        out[0] = mine[c]
        out[1] = right[c]
        out[2] = across[...]
        out[3] = left[c]


def stack_chunks(mine, right, passed, left):
    _, rows, width = mine.shape
    return pl.pallas_call(
        stack_kernel,
        out_shape=[jax.ShapeDtypeStruct((4, rows, width), bf16)] * CHUNKS,
        compiler_params=pltpu.CompilerParams(vmem_limit_bytes=LARGE),
        cost_estimate=pl.CostEstimate(flops=STACK << 30, bytes_accessed=6 << 20, transcendentals=0),
    )(mine, right, *passed, left)


def slots_of(subset_ids, owner_rows, vocab_count, capacity):
    count = subset_ids.shape[0]
    owner_of = subset_ids // owner_rows
    onehot = (owner_of[:, None] == jnp.arange(vocab_count)[None, :]).astype(bf16)
    earlier = (jnp.arange(count)[:, None] > jnp.arange(count)[None, :]).astype(bf16)
    before = matmul(earlier, onehot, 1, 0)
    rank = jnp.sum(before * onehot.astype(f32), axis=1).astype(i32)
    return owner_of * capacity + rank, subset_ids % owner_rows


def on_device(hidden, table, subset_ids, targets):
    nx, nc, ny, nz = (lax.axis_size(a) for a in ("x", "core", "y", "z"))
    x, core, y = (lax.axis_index(a) for a in ("x", "core", "y"))
    pos = jnp.stack([x, core, y]).astype(i32)
    vocab_count = ny * nz
    positions, width = hidden.shape
    owner_rows = table.shape[0]
    sub_dev = subset_ids.shape[0]
    pos_dev = targets.shape[0]
    capacity = 2 * sub_dev // vocab_count
    slots = vocab_count * capacity
    out_pos = positions // vocab_count
    small = out_pos // CHUNKS
    rows = pos_dev // CHUNKS

    table_far = lax.ppermute(table, "core", SWAP)
    ordered = hidden.reshape(nx, nc, pos_dev // out_pos, CHUNKS, small, width)
    ordered = ordered.transpose(3, 0, 1, 2, 4, 5).reshape(CHUNKS, nx, nc, rows, width)
    far = lax.dynamic_index_in_dim(ordered, 1 - core, 2, keepdims=False)
    far = lax.ppermute(far, "core", SWAP)

    targets = targets.reshape(pos_dev // out_pos, CHUNKS, small, sub_dev)
    targets = targets.transpose(1, 0, 2, 3).reshape(pos_dev, sub_dev)
    slot_index, local_row = slots_of(subset_ids, owner_rows, vocab_count, capacity)
    to_slot = (jnp.arange(slots)[:, None] == slot_index[None, :]).astype(bf16)
    line = lax.broadcasted_iota(i32, (-pos_dev % 128 or 128, 1), 0)
    side = jnp.where(line == 0, local_row // LOW, jnp.where(line == 1, local_row % LOW, line == 2))
    sent = jnp.concatenate([targets, side.astype(bf16)], axis=0)
    payload = matmul(to_slot, sent, 1, 1, bf16)
    payload, far = lax.optimization_barrier((payload, far))
    got = lax.all_to_all(
        payload.reshape(vocab_count, capacity, -1), VOCAB, split_axis=0, concat_axis=0, tiled=True
    ).reshape(slots, -1)

    parts = []
    for c in range(CHUNKS):
        if c:
            far, parts[0][0] = lax.optimization_barrier((far, parts[0][0]))
        *codes, own = partial_logits(pos, ordered, far, table, table_far, c)
        parts.append(
            [own] + [lax.ppermute(codes[k - 1], "x", shift("x", k)) for k in (2, 1, 3)]
        )

    logits = [sum_codes(parts[0][0], parts[0][1:])]
    got, later, logits[0] = lax.optimization_barrier((got, ordered, logits[0]))
    info = got[:, pos_dev : pos_dev + 3].astype(i32)
    row_of = jnp.where(info[:, 2] > 0, info[:, 0] * LOW + info[:, 1], -1)
    to_row = (row_of[:, None] == jnp.arange(owner_rows)[None, :]).astype(bf16)
    landed = matmul(got, to_row, 0, 0)
    chosen = landed[pos_dev + 2 : pos_dev + 3] > 0.5

    order = [lax.dynamic_index_in_dim(later, (x + j) % nx, 1, False) for j in range(nx)]
    order = jnp.stack(order, 1)
    order = [lax.dynamic_index_in_dim(order, i, 2, False) for i in (core, 1 - core)]
    order = jnp.stack(order, 1).reshape(positions, width)
    order, *parts[1] = lax.optimization_barrier((order, *parts[1]))
    local = []
    for c in range(CHUNKS):
        if c:
            *parts[c], local[-1] = lax.optimization_barrier((*parts[c], local[-1]))
            logits.append(sum_codes(parts[c][0], parts[c][1:]))
        here = logits[c]
        peak = jnp.max(jnp.where(chosen, here, FAR), axis=1)
        total = jnp.sum(jnp.where(chosen, jnp.exp(here - peak[:, None]), 0.0), axis=1)
        local.append(jnp.stack([peak, total, jnp.sum(landed[c * rows : (c + 1) * rows], axis=1)]))
    stats = jnp.stack(local).reshape(1, CHUNKS * 3 * rows)
    stats = jnp.broadcast_to(stats, (vocab_count,) + stats.shape[1:])
    stats = lax.all_to_all(stats, VOCAB, split_axis=0, concat_axis=0, tiled=True)
    stats = stats.reshape(vocab_count, CHUNKS, 3, rows)
    row_peak = jnp.max(stats[:, :, 0], axis=0)
    row_total = jnp.sum(stats[:, :, 1] * jnp.exp(stats[:, :, 0] - row_peak[None]), axis=0)
    row_mass = jnp.sum(stats[:, :, 2], axis=0)
    mine = []
    for c in range(CHUNKS):
        probs = jnp.exp(logits[c] - row_peak[c][:, None]) / row_total[c][:, None]
        grad = LOSS_SCALE * (probs * row_mass[c][:, None] - landed[c * rows : (c + 1) * rows])
        mine.append(jnp.where(chosen, grad, 0.0).astype(bf16))
    mine = jnp.stack(mine)

    out = matmul(to_row, jnp.concatenate(logits, axis=0).astype(bf16), 1, 1, bf16)

    right = lax.ppermute(mine, "x", shift("x", -1))
    left = lax.ppermute(mine, "x", shift("x", 1))
    passed = [
        lax.ppermute(right[0], "x", shift("x", -1)),
        lax.ppermute(left[1], "x", shift("x", 1)),
    ]
    back = lax.all_to_all(
        out.reshape(vocab_count, capacity, pos_dev), VOCAB, split_axis=0, concat_axis=0, tiled=True
    ).reshape(slots, pos_dev)
    stacked = stack_chunks(mine, right, passed, left)
    back, *stacked = lax.optimization_barrier((back, *stacked))
    pieces, terms = [], []
    for c, here in enumerate(stacked):
        there = lax.ppermute(here, "core", SWAP)
        terms += [here, there]
        if c:
            pieces[0][0], there = lax.optimization_barrier((pieces[0][0], there))
        *sent, own = hidden_parts(pos, (here, there), table, True)
        pieces.append(
            [own, [lax.ppermute(sent[k - 1], "y", shift("y", k)) for k in (2, 1, 3)]]
        )
    (pieces[0][0], pieces[1][0]) = lax.optimization_barrier((pieces[0][0], pieces[1][0]))
    grads = jnp.concatenate(terms).reshape(positions, -1)
    grads, *pieces[0][1] = lax.optimization_barrier((grads, *pieces[0][1]))
    first = add_and_code(*pieces[0], nz)
    first, grads = lax.optimization_barrier((first, grads))
    table_grad = matmul(grads, order, 0, 0, bf16)
    pieces = [first, add_and_code(*pieces[1], nz, (table_grad,))]
    pieces = [lax.all_to_all(p, "z", split_axis=0, concat_axis=0, tiled=True) for p in pieces]
    pieces = [jnp.sum(decode(p), axis=0).astype(bf16) for p in pieces]
    hidden_grad = jnp.concatenate(pieces, axis=0)

    draft = matmul(back, to_slot, 0, 0, bf16)
    draft = draft.reshape(CHUNKS, pos_dev // out_pos, small, sub_dev).transpose(1, 0, 2, 3)
    return draft.reshape(pos_dev, sub_dev), hidden_grad, table_grad


def solution(mesh):
    fine = Mesh(mesh.devices.reshape(4, 2, 4, 8), ROWS + VOCAB)
    return jax.shard_map(
        on_device,
        mesh=fine,
        in_specs=(P(None, ROWS), P(VOCAB, ROWS), P(VOCAB), P(ROWS, VOCAB)),
        out_specs=(P(ROWS, VOCAB), P(VOCAB, ROWS), P(VOCAB, ROWS)),
        check_vma=False,
    )
```
